128 devices in a mesh: shard: 32 (over x, y, core), rep: 4 (over z).
Axes of the slice: x: 4, y: 4, z: 4, core: 2. Of those that a mesh axis runs over, the one named last changes fastest.
Arguments:
- embeddings: float32 [65536, 768], P(('shard', 'rep')), may hold values from -6 to 6
- destination: int32 [65536, 1], P(('shard', 'rep')), may hold values from 0 to 127; in each aligned block of 512 rows (0 to 511, 512 to 1023, ...) at most 8 rows name the same one
- labels: int32 [65536], P(('shard', 'rep')), may hold values from 0 to 127
- old_centroids: float32 [16384, 768], P(('shard', 'rep')), may hold values from -6 to 6
- codebook: float32 [128, 256, 6], P('rep'), may hold values from -6 to 6
Outputs:
- new_centroids: float32 [16384, 768], P(('shard', 'rep'))
- distortion: float32 [128, 131072], P('rep', 'shard')
The draws below stay inside these ranges and needn't reach their ends.
Inputs may be any that keep to these rules, and one draw needn't show every extreme that they name: Among the rows of one owner, no destination is named more than 8 times, a bound that some block reaches.
All inputs are finite; a program needn't handle non-finite values.
Results may differ from the reference program's by a relative error of at most 0.0003.
Values sent between devices are 32-bit elements; how exact they have to be, the bound alone decides.
No kernel may reach another device: no remote copies, remote signals or barrier semaphores. Data moves between devices by JAX's collectives and lax.ppermute only.
A program may use at most 64 MiB of HBM per device.

```python
import math
from functools import partial
import jax
import jax.numpy as jnp
import numpy as np
from jax import lax

D = 768
DSUB = 6
K = 256
ROWS_DEV = 512
P_DEV = 128
M = 128
CAP = 8
ROWS = 65536
POSTINGS = 16384
N_SHARD = 32
N_REP = 4
DEVICES = 128


def plant(result, key, low, top_value):
    extent = result.shape
    index_at = [jax.random.randint(jax.random.fold_in(key, axis), (), 0, extent[axis]) for axis in range(len(extent))]
    result = result.at[tuple(index_at)].set(low)
    longest = extent.index(max(extent))
    index_at[longest] = (index_at[longest] + 1) % extent[longest]
    return result.at[tuple(index_at)].set(top_value)


def block_scale(stream_key, extent, pieces, smallest, top_value):
    factor_of, own = 1.0, jax.random.fold_in(stream_key, 6)
    for dim, blocks in pieces:
        draws = jnp.exp(jax.random.uniform(jax.random.fold_in(own, dim), (blocks,), jnp.float32, smallest / len(pieces), top_value / len(pieces)))
        factor_of = factor_of * jnp.repeat(draws, extent[dim] // blocks).reshape([-1 if axis == dim else 1 for axis in range(len(extent))])
    return factor_of


def deal_out(key, own, number, rows, amount, top, bound, skew):
    ranking = jax.random.permutation(key, amount)
    heavy_load, usual = portions_of(amount, rows * top, bound, skew, True), portions_of(amount, rows * top, bound, skew, False)
    places = jnp.arange(amount)

    def named(tallies, rotation):
        used = int((tallies > 0).sum())
        fixed = max(1, used // 4)
        shifted = fixed + (places - fixed + rotation * (used - fixed)) % max(1, amount - fixed)
        return jnp.zeros((amount,), jnp.int32).at[ranking[jnp.where(places < fixed, places, shifted)]].set(jnp.asarray(tallies, jnp.int32))

    tallies = jnp.where(number % 4 == 0, named(heavy_load, number // 4), named(usual, number - number // 4 - 1))
    mixed = jax.random.permutation(jax.random.fold_in(own, 3), amount)
    source_of, sink = mixed[0:amount // 2 * 2:2], mixed[1:amount // 2 * 2:2]
    room = jnp.minimum(tallies[source_of] - 1, bound - tallies[sink]) // 2
    room = jnp.where((source_of == ranking[0]) | (sink == ranking[0]) | (tallies[sink] == 0), 0, jnp.maximum(room, 0))
    shifted = jax.random.randint(jax.random.fold_in(own, 4), (amount // 2,), 0, 1 << 20) % (room + 1)
    tallies = tallies.at[source_of].add(-shifted).at[sink].add(shifted)
    items = jnp.searchsorted(jnp.cumsum(tallies), jnp.arange(rows * top), side="right").astype(jnp.int32)
    table = items.reshape(top, rows).T
    table = table[jax.random.permutation(jax.random.fold_in(own, 1), rows)]
    rotation = jax.random.randint(jax.random.fold_in(own, 2), (rows, 1), 0, top)
    return jnp.take_along_axis(table, (jnp.arange(top)[None, :] + rotation) % top, axis=1)


def portions_of(number_of, total, bound, skew, full):
    loads = [(1 << 20) // math.isqrt(standing ** skew) + 1 for standing in range(1, number_of + 1)]
    largest = bound if full else min(bound, max(-(-total // number_of), total * loads[0] // sum(loads)))
    least = 1 if total - largest >= number_of - 1 else 0
    holding, spare = [largest] + [least] * (number_of - 1), total - largest - least * (number_of - 1)
    while spare > 0:
        free = [i for i in range(1, number_of) if holding[i] < largest] or [i for i in range(1, number_of) if holding[i] < bound]
        whole, left = sum([loads[i] for i in free]), spare
        for i in free:
            more = min(bound - holding[i], max(1, left * loads[i] // whole), spare)
            holding[i] = holding[i] + more
            spare = spare - more
    return np.array(holding)


def bell_draw(rng, extent, deviation, reach, shards=(), held_as=jnp.bfloat16):
    array = deviation * jax.random.normal(rng, extent, jnp.float32)
    if shards:
        array = array * block_scale(rng, extent, shards, -0.22, 0.18)
    return jnp.clip(array, -reach, reach).astype(held_as)


def setup_inputs(seed: int = 0) -> dict:
    arg_keys = jax.random.split(jax.random.key(seed), 6)
    embeddings = bell_draw(arg_keys[0], (ROWS, D), 1.0, 6.0, ((0, 128),), jnp.float32)
    destination_keys = jax.random.split(jax.random.fold_in(arg_keys[1], 1), ROWS // ROWS_DEV)
    destination_turns = jax.random.permutation(jax.random.fold_in(arg_keys[1], 3), ROWS // ROWS_DEV)
    destination = jax.vmap(lambda own, number: deal_out(jax.random.fold_in(arg_keys[1], 2), own, number, ROWS_DEV, DEVICES, 1, CAP, 2))(destination_keys, destination_turns).reshape((ROWS, 1))
    labels = plant(jax.random.randint(arg_keys[2], (ROWS,), 0, P_DEV), jax.random.fold_in(arg_keys[2], 1), 0, P_DEV - 1).astype(jnp.int32)
    old_centroids = bell_draw(arg_keys[3], (POSTINGS, D), 1.0, 6.0, ((0, 128),), jnp.float32)
    codebook = bell_draw(arg_keys[4], (M, K, DSUB), 1.0, 6.0, ((0, 4),), jnp.float32)
    return {"embeddings": embeddings, "destination": destination, "labels": labels, "old_centroids": old_centroids, "codebook": codebook}


prior_weight = 8.0


def positions(targets_row, owners):
    indicator = (targets_row[:, None] == jnp.arange(owners, dtype=jnp.int32)[None, :]).astype(jnp.int32)
    return jnp.sum((jnp.cumsum(indicator, axis=0) - 1) * indicator, axis=1).astype(jnp.int32)


def rebalance(block_rows, block_labels, previous):
    indicator = (block_labels[:, None] == jnp.arange(previous.shape[0], dtype=jnp.int32)[None, :]).astype(jnp.float32)
    sums = jnp.dot(indicator.T, block_rows, precision=lax.Precision.HIGHEST, preferred_element_type=jnp.float32)
    counts = jnp.sum(indicator, axis=0)
    centroids = (prior_weight * previous + sums) / (prior_weight + counts)[:, None]
    residual = block_rows - jnp.dot(indicator, centroids, precision=lax.Precision.HIGHEST, preferred_element_type=jnp.float32)
    return centroids, residual


def distortion(residual, book):
    row_count = residual.shape[0]
    sub_count = book.shape[0]
    sub_dim = book.shape[2]
    block_width = max(1, min(sub_count, 32768 // row_count))
    while sub_count % block_width:
        block_width -= 1
    block_count = sub_count // block_width
    subvectors = residual.reshape(row_count, block_count, block_width, sub_dim).transpose(1, 0, 2, 3)
    book_blocks = book.reshape(block_count, block_width, book.shape[1], sub_dim)

    def block_distortion(operands):
        segment, codewords = operands
        inner_term = jnp.einsum("rmd,mkd->mrk", segment, codewords, precision=lax.Precision.HIGHEST)
        row_norms = jnp.sum(segment * segment, axis=-1).T
        word_norms = jnp.sum(codewords * codewords, axis=-1)
        return jnp.min(row_norms[:, :, None] - 2.0 * inner_term + word_norms[:, None, :], axis=2)

    result_blocks = lax.map(block_distortion, (subvectors, book_blocks))
    return result_blocks.reshape(sub_count, row_count)


def reference(embeddings, destination, labels, old_centroids, codebook):
    owners = N_SHARD * N_REP
    capacity = 2 * ROWS_DEV // owners
    slot_count = owners * capacity
    targets = destination[:, 0].reshape(owners, ROWS_DEV)
    position = jax.vmap(partial(positions, owners=owners))(targets)
    sources = jnp.arange(owners, dtype=jnp.int32)[:, None]
    placement_index = (targets * slot_count + sources * capacity + position).reshape(-1).astype(jnp.int32)
    received = jnp.zeros((owners * slot_count, D), jnp.float32).at[placement_index].set(embeddings)
    received_labels = jnp.full((owners * slot_count,), -1, jnp.int32).at[placement_index].set(labels)

    def per_owner(operands):
        block_rows, block_labels, previous = operands
        centroids, residual = rebalance(block_rows, block_labels, previous)
        return centroids, distortion(residual, codebook)

    centroids, scores = lax.map(per_owner, (received.reshape(owners, slot_count, D), received_labels.reshape(owners, slot_count), old_centroids.reshape(owners, P_DEV, D)))
    new_centroids = centroids.reshape(owners * P_DEV, D)
    scores = scores.transpose(1, 0, 2).reshape(M, owners * slot_count)
    return new_centroids, scores
```

```python
import functools
import jax
import jax.numpy as jnp
from jax import lax
from jax.experimental import pallas as pl
from jax.experimental.pallas import tpu as pltpu
from jax.sharding import PartitionSpec as P

prior_weight = 8.0
F32 = jnp.float32
BF16 = jnp.bfloat16
VMEM = pl.BlockSpec(memory_space=pltpu.VMEM)
SMEM = pl.BlockSpec(memory_space=pltpu.SMEM)
LIMIT = 56 * 2**20
MSG = 49


def split3(x):
    first = x.astype(BF16)
    rest = x - first.astype(F32)
    second = rest.astype(BF16)
    third = (rest - second.astype(F32)).astype(BF16)
    return first, second, third


def iota(shape, dim):
    return lax.broadcasted_iota(jnp.int32, shape, dim)


def dot(a, b):
    return jnp.dot(a, b, preferred_element_type=F32)


def pack_kernel(dest_ref, label_ref, rows_ref, out_ref, a_ref, b_ref):
    dest = dest_ref[...]
    named = (iota((128, 512), 0) == dest).astype(F32)
    earlier = (iota((512, 512), 0) < iota((512, 512), 1)).astype(BF16)
    before = dot(named.astype(BF16), earlier)
    slot = dest * 8 + jnp.sum(named * before, axis=0, keepdims=True).astype(jnp.int32)

    group = (iota((32, 512), 0) == slot // 32).astype(F32)
    within = (iota((128, 512), 0) == slot % 32).astype(BF16)
    labels = group * (label_ref[...] + 1).astype(F32)
    label_rows = lax.dot_general(
        labels.astype(BF16), within, (((1,), (1,)), ((), ())), preferred_element_type=F32
    ) - 1.0
    for quarter in range(4):
        out_ref[pl.ds(MSG * quarter + 48, 32, stride=4 * MSG), :] = label_rows

    low = iota((512, 128), 1) < 64
    tile = [rows_ref[:, 128 * i : 128 * i + 128] for i in range(6)]
    wide = [
        tile[0],
        pltpu.roll(jnp.where(low, tile[2], tile[1]), 64, 1),
        tile[3],
        pltpu.roll(jnp.where(low, tile[5], tile[4]), 64, 1),
    ]
    narrow = [jnp.where(low, tile[1], tile[2]), jnp.where(low, tile[4], tile[5])]
    for i, block in enumerate(wide + narrow):
        for piece, part in enumerate(split3(block)):
            a_ref[512 * piece : 512 * piece + 512, 128 * i : 128 * i + 128] = part

    for half in range(2):
        pick = (iota((512, 512), 0) + 512 * half == slot).astype(BF16)
        b_ref[...] = (
            dot(pick, a_ref[0:512, :]) + dot(pick, a_ref[512:1024, :]) + dot(pick, a_ref[1024:1536, :])
        )
        lower = iota((8, 128), 1) < 64
        for s in range(16):
            for quarter in range(4):
                base = MSG * (4 * (16 * half + s) + quarter)
                out_ref[pl.ds(base, 32), :] = b_ref[32 * s : 32 * s + 32, 128 * quarter : 128 * quarter + 128]
                lanes = 512 + 128 * (quarter // 2)
                for pair in range(2):
                    one = b_ref[32 * s + 8 * pair : 32 * s + 8 * pair + 8, lanes : lanes + 128]
                    two = b_ref[32 * s + 8 * pair + 16 : 32 * s + 8 * pair + 24, lanes : lanes + 128]
                    if quarter % 2 == 0:
                        both = jnp.where(lower, one, pltpu.roll(two, 64, 1))
                    else:
                        both = jnp.where(lower, pltpu.roll(one, 64, 1), two)
                    out_ref[pl.ds(base + 32 + 8 * pair, 8), :] = both


def quarters_kernel(rep_ref, old_ref, own_ref, one_ref, two_ref, three_ref):
    rep = rep_ref[0]
    low = iota((128, 128), 1) < 64
    tile = [old_ref[:, 128 * i : 128 * i + 128] for i in range(6)]
    wide = [
        tile[0],
        pltpu.roll(jnp.where(low, tile[2], tile[1]), 64, 1),
        tile[3],
        pltpu.roll(jnp.where(low, tile[5], tile[4]), 64, 1),
    ]
    narrow = [tile[1], pltpu.roll(tile[2], 64, 1), tile[4], pltpu.roll(tile[5], 64, 1)]
    for step, ref in enumerate((own_ref, one_ref, two_ref, three_ref)):
        which = lax.rem(rep + step, 4)
        for start, choice in ((0, wide), (128, narrow)):
            ref[:, start : start + 128] = jnp.where(
                which == 0,
                choice[0],
                jnp.where(which == 1, choice[1], jnp.where(which == 2, choice[2], choice[3])),
            )


def book_kernel(book_ref, out_ref):
    row = iota((256, 256), 0)
    for g in range(4):
        words = book_ref[:, 8 * g : 8 * g + 8, :].reshape(48, 256)
        norm = jnp.sum((words * words).reshape(6, 8, 256), axis=0)
        first, second, third = (part.astype(F32) for part in split3(-2.0 * words))
        n1, n2, n3 = (part.astype(F32) for part in split3(norm))
        stack = jnp.concatenate([first, second, first, second, first], axis=0)
        for m in range(8):
            mine = jnp.where(iota((240, 256), 0) % 8 == m, stack, 0.0)
            tail_row = iota((16, 256), 0)
            tail = jnp.where(
                tail_row == 0,
                n1[m : m + 1],
                jnp.where(tail_row == 1, n2[m : m + 1], jnp.where(tail_row == 2, n3[m : m + 1], 0.0)),
            )
            out_ref[8 * g + m] = jnp.concatenate([mine, tail], axis=0).T.astype(BF16)


def centroid_kernel(rep_ref, got_ref, own_ref, one_ref, two_ref, three_ref, cent_ref, turned_ref, lab_ref):
    rep = rep_ref[0]
    lab = got_ref[pl.ds(48, 128, stride=MSG), :].astype(BF16)
    spread = (iota((128, 512), 0) == (iota((128, 512), 1) // 128) * 8 + iota((128, 512), 1) % 8).astype(BF16)
    moved = dot(lab, spread)
    keep = iota((128, 512), 0) % 16 == (iota((128, 512), 1) % 128) // 8
    lab_rows = jnp.sum(jnp.where(keep, moved, 0.0).reshape(8, 16, 512), axis=1)
    lab_ref[...] = lab_rows

    posting = iota((128, 128), 0).astype(F32)
    low = iota((128, 128), 1) < 64
    for pair in range(2):
        sums = [jnp.zeros((128, 256), F32), jnp.zeros((128, 256), F32)]
        counts = [jnp.zeros((128, 128), F32), jnp.zeros((128, 128), F32)]
        for c in range(8):
            senders = range(16 * c, 16 * c + 16)
            narrow = jnp.concatenate([got_ref[pl.ds(MSG * q + 32 + 8 * pair, 8), :] for q in senders], axis=0)
            narrow_parts = split3(narrow)
            narrow_turned = narrow.T
            for k in range(2):
                r = pair + 2 * k
                wide = jnp.concatenate([got_ref[pl.ds(MSG * q + 8 * r, 8), :] for q in senders], axis=0)
                hot = (posting == lab_rows[c : c + 1, 128 * r : 128 * r + 128]).astype(F32)
                counts[k] += hot
                hot = hot.astype(BF16)
                for part, other in zip(split3(wide), narrow_parts):
                    sums[k] += dot(hot, jnp.concatenate([part, other], axis=1))
                turned_ref[8 * r + c, 0:128, :] = wide.T
                turned_ref[8 * r + c, 128:192, :] = narrow_turned[64 * k : 64 * k + 64]
        for k in range(2):
            r = pair + 2 * k
            step = lax.rem(rep - r + 4, 4)
            weight = prior_weight + jnp.sum(counts[k], axis=1, keepdims=True)
            for start in (0, 128):
                total = sums[k][:, start : start + 128]
                if start and k:
                    total = pltpu.roll(total, 64, 1)
                olds = [ref[:, start : start + 128] for ref in (own_ref, one_ref, two_ref, three_ref)]
                old = jnp.where(
                    step == 0, olds[0], jnp.where(step == 1, olds[1], jnp.where(step == 2, olds[2], olds[3]))
                )
                new = (prior_weight * old + total) / weight
                if start:
                    new = jnp.where(low, new, 0.0)
                cent_ref[r, :, start : start + 128] = new


def score_kernel(turned_ref, cent_ref, lab_ref, book_ref, out_ref, flip_ref, cent3_ref, res_ref, norm_ref):
    for r in range(4):
        flip_ref[0:128, :] = cent_ref[r, :, 0:128].T
        flip_ref[128:256, :] = cent_ref[r, :, 128:256].T
        for g in range(4):
            for t in range(6):
                rows = flip_ref[pl.ds(48 * g + t, 8, stride=6), :]
                for piece, part in enumerate(split3(rows)):
                    cent3_ref[4 * r + g, 48 * piece + 8 * t : 48 * piece + 8 * t + 8, :] = part.astype(F32)
    ones = jnp.where(iota((16, 1024), 0) < 3, 1.0, 0.0).astype(BF16)
    res_ref[0, 240:256, :] = ones
    res_ref[1, 240:256, :] = ones

    def prepare(i, buffer):
        r = i // 4
        g = i % 4
        labs = lab_ref[:, pl.ds(pl.multiple_of(128 * r, 128), 128)]
        posting = iota((128, 128), 0).astype(F32)
        hot = jnp.concatenate([(posting == labs[c : c + 1]).astype(BF16) for c in range(8)], axis=1)
        part = dot(cent3_ref[i].astype(BF16), hot)
        near = part[0:48] + part[48:96] + part[96:144]
        rows = jnp.concatenate(
            [
                jnp.concatenate(
                    [turned_ref[8 * r + c, pl.ds(48 * g + t, 8, stride=6), :] for c in range(8)], axis=1
                )
                for t in range(6)
            ],
            axis=0,
        )
        res = rows - near
        norm_ref[buffer] = jnp.sum((res * res).reshape(6, 8, 1024), axis=0)
        first, second, third = split3(res)
        res_ref[buffer, 0:48, :] = first
        res_ref[buffer, 48:96, :] = first
        res_ref[buffer, 96:144, :] = second
        res_ref[buffer, 144:192, :] = second
        res_ref[buffer, 192:240, :] = third

    def score(i, buffer):
        r = i // 4
        g = i % 4
        right = res_ref[buffer]
        best = []
        for m in range(8):
            value = dot(book_ref[8 * g + m], right)
            value = jnp.min(value.reshape(32, 8, 1024), axis=0)
            best.append(jnp.min(value, axis=0, keepdims=True))
        out_ref[pl.ds(pl.multiple_of(8 * g, 8), 8), pl.ds(pl.multiple_of(1024 * r, 1024), 1024)] = (
            jnp.concatenate(best, axis=0) + norm_ref[buffer]
        )

    prepare(0, 0)

    def step(i, carry):
        score(i, i % 2)
        prepare(jnp.minimum(i + 1, 15), (i + 1) % 2)
        return carry

    lax.fori_loop(0, 16, step, 0)


def join_kernel(got_ref, out_ref):
    low = iota((128, 128), 1) < 64
    for half in range(2):
        wide0, narrow0 = got_ref[2 * half, :, 0:128], got_ref[2 * half, :, 128:256]
        wide1, narrow1 = got_ref[2 * half + 1, :, 0:128], got_ref[2 * half + 1, :, 128:256]
        turned = pltpu.roll(wide1, 64, 1)
        at = 384 * half
        out_ref[:, at : at + 128] = wide0
        out_ref[:, at + 128 : at + 256] = jnp.where(low, narrow0, turned)
        out_ref[:, at + 256 : at + 384] = jnp.where(low, turned, pltpu.roll(narrow1, 64, 1))


def call(kernel, out_shape, specs, scratch=(), flops=0, moved=0):
    many = isinstance(out_shape, (tuple, list))
    return pl.pallas_call(
        kernel,
        out_shape=out_shape,
        in_specs=specs,
        out_specs=[VMEM] * len(out_shape) if many else VMEM,
        scratch_shapes=scratch,
        compiler_params=pltpu.CompilerParams(vmem_limit_bytes=LIMIT),
        cost_estimate=pl.CostEstimate(flops=flops, bytes_accessed=moved, transcendentals=0),
    )


def shape(*dims, dtype=F32):
    return jax.ShapeDtypeStruct(dims, dtype)


def local(embeddings, destination, labels, old_centroids, codebook):
    rep = lax.axis_index("rep").astype(jnp.int32).reshape(1)
    outgoing = call(
        pack_kernel,
        shape(128 * MSG, 128),
        [VMEM] * 3,
        [pltpu.VMEM((1536, 768), BF16), pltpu.VMEM((512, 768), F32)],
        flops=2 * 1024 * 512 * 768 * 3,
        moved=5 * 2**20,
    )(destination.reshape(1, 512), labels.reshape(1, 512), embeddings)
    received = lax.all_to_all(
        outgoing.reshape(128, 1, MSG * 128), ("shard", "rep"), split_axis=0, concat_axis=0, tiled=True
    ).reshape(128 * MSG, 128)

    quarters = call(
        quarters_kernel, [shape(128, 256)] * 4, [SMEM, VMEM], flops=2**20, moved=2**20
    )(rep, old_centroids)
    olds = [quarters[0]]
    for step in (1, 2, 3):
        olds.append(lax.ppermute(quarters[step], "rep", [(i, (i + step) % 4) for i in range(4)]))
    book = call(
        book_kernel, shape(32, 256, 256, dtype=BF16), [VMEM], flops=2**28, moved=5 * 2**20
    )(jnp.transpose(codebook, (2, 0, 1)))

    cents, turned, lab_rows = call(
        centroid_kernel,
        [shape(4, 128, 256), shape(32, 192, 128), shape(8, 512)],
        [SMEM] + [VMEM] * 5,
        flops=2 * 128 * 4096 * 256 * 3,
        moved=7 * 2**20,
    )(rep, received, *olds)
    returned = lax.all_to_all(cents, "rep", split_axis=0, concat_axis=0, tiled=True)
    scores = call(
        score_kernel,
        shape(32, 4096),
        [VMEM] * 4,
        [
            pltpu.VMEM((256, 128), F32),
            pltpu.VMEM((16, 144, 128), F32),
            pltpu.VMEM((2, 256, 1024), BF16),
            pltpu.VMEM((2, 8, 1024), F32),
        ],
        flops=2 * 131072 * 256 * 256,
        moved=8 * 2**20,
    )(turned, cents, lab_rows, book)
    centroids = call(join_kernel, shape(128, 768), [VMEM], flops=2**18, moved=2**20)(returned)
    return (centroids, scores)


def solution(mesh):
    placed = (
        P(("shard", "rep"), None),
        P(("shard", "rep"), None),
        P(("shard", "rep")),
        P(("shard", "rep"), None),
        P("rep", None, None),
    )
    return jax.shard_map(
        local,
        mesh=mesh,
        in_specs=placed,
        out_specs=(P(("shard", "rep"), None), P("rep", "shard")),
        check_vma=False,
    )
```

```python
import functools
import jax
import jax.numpy as jnp
from jax import lax
from jax.experimental import pallas as pl
from jax.experimental.pallas import tpu as pltpu
from jax.sharding import PartitionSpec as P

prior_weight = 8.0
F32 = jnp.float32
BF16 = jnp.bfloat16
VMEM = pl.BlockSpec(memory_space=pltpu.VMEM)
SMEM = pl.BlockSpec(memory_space=pltpu.SMEM)
HBM = pl.BlockSpec(memory_space=pltpu.HBM)
DMA = pltpu.SemaphoreType.DMA
LIMIT = 58 * 2**20

ALL = {"owners": (0, 1, 2, 3), "narrow": (((0, 1), 32), ((2, 3), 40)), "labels": 48, "rows": 49}


def split2(x):
    first = x.astype(BF16)
    return first, (x - first.astype(F32)).astype(BF16)


def split3(x):
    first, second = split2(x)
    third = (x - first.astype(F32) - second.astype(F32)).astype(BF16)
    return first, second, third


def iota(shape, dim):
    return lax.broadcasted_iota(jnp.int32, shape, dim)


def dot(a, b):
    return jnp.dot(a, b, preferred_element_type=F32)


def pack_kernel(
    chunk, parts, dest_hbm, label_hbm, rows_hbm, out_hbm, dest_ref, label_ref, rows_ref, out_ref, a_ref, b_ref, sem
):
    owners, message = chunk["owners"], chunk["rows"]
    count = len(owners)
    loads = [
        pltpu.make_async_copy(src, dst, sem.at[i])
        for i, (src, dst) in enumerate(((dest_hbm, dest_ref), (label_hbm, label_ref), (rows_hbm, rows_ref)))
    ]
    for load in loads:
        load.start()
    loads[0].wait()
    dest = dest_ref[...]
    named = (iota((128, 512), 0) == dest).astype(F32)
    earlier = (iota((512, 512), 0) < iota((512, 512), 1)).astype(BF16)
    before = dot(named.astype(BF16), earlier)
    spot = jnp.sum(named * before, axis=0, keepdims=True).astype(jnp.int32)
    shard, owner = dest // 4, dest % 4
    place = (owner - owners[0]) * 8 + spot
    chosen = (owner >= owners[0]) & (owner <= owners[-1])
    slot = jnp.where(chosen, shard * (8 * count) + place, -1)

    loads[1].wait()
    if chunk["labels"] is not None:
        group = (iota((32, 512), 0) == shard).astype(F32)
        within = (iota((128, 512), 0) == owner * 8 + spot).astype(BF16)
        labels = group * (label_ref[...] + 1).astype(F32)
        label_rows = lax.dot_general(
            labels.astype(BF16), within, (((1,), (1,)), ((), ())), preferred_element_type=F32
        ) - 1.0
        for quarter in range(4):
            out_ref[pl.ds(message * quarter + chunk["labels"], 32, stride=4 * message), :] = label_rows

    loads[2].wait()
    low = iota((512, 128), 1) < 64
    tile = [rows_ref[:, 128 * i : 128 * i + 128] for i in range(6)]
    wide = [
        tile[0],
        pltpu.roll(jnp.where(low, tile[2], tile[1]), 64, 1),
        tile[3],
        pltpu.roll(jnp.where(low, tile[5], tile[4]), 64, 1),
    ]
    narrow = [jnp.where(low, tile[1], tile[2]), jnp.where(low, tile[4], tile[5])]
    for i, block in enumerate(wide + narrow):
        for piece, part in enumerate(split2(block)):
            a_ref[512 * piece : 512 * piece + 512, 128 * i : 128 * i + 128] = part

    lower = iota((8, 128), 1) < 64
    stores = []
    groups = 32 // parts
    for part in range(parts):
        size = groups * 8 * count
        pick = (iota((size, 512), 0) + size * part == slot).astype(BF16)
        got = b_ref.at[part % 2]
        got[...] = dot(pick, a_ref[0:512, :]) + dot(pick, a_ref[512:1024, :])
        for s in range(groups):
            for quarter in range(4):
                base = message * (4 * (groups * part + s) + quarter)
                at = 8 * count * s
                out_ref[pl.ds(base, 8 * count), :] = got[at : at + 8 * count, 128 * quarter : 128 * quarter + 128]
                lanes = 512 + 128 * (quarter // 2)
                for members, offset in chunk["narrow"]:
                    rows = [at + 8 * (r - owners[0]) for r in members]
                    one = got[rows[0] : rows[0] + 8, lanes : lanes + 128]
                    if len(members) == 2:
                        two = got[rows[1] : rows[1] + 8, lanes : lanes + 128]
                    else:
                        two = pltpu.roll(one, 4, 0)
                    if quarter % 2 == 0:
                        both = jnp.where(lower, one, pltpu.roll(two, 64, 1))
                    else:
                        both = jnp.where(lower, pltpu.roll(one, 64, 1), two)
                    height = 4 * len(members)
                    out_ref[pl.ds(base + offset, height), :] = both[0:height]
        span = pl.ds(128 * message // parts * part, 128 * message // parts)
        stores.append(pltpu.make_async_copy(out_ref.at[span], out_hbm.at[span], sem.at[3 + part]))
        stores[-1].start()
    for store in stores:
        store.wait()


def fold(block):
    return jnp.where(iota((64, 128), 1) < 64, block[0:64], pltpu.roll(block[64:128], 64, 1))


def unfold(block):
    return jnp.concatenate([block, pltpu.roll(block, 64, 1)], axis=0)


def quarters_kernel(rep_ref, old_ref, own_ref, one_ref, two_ref, three_ref):
    rep = rep_ref[0]
    low = iota((128, 128), 1) < 64
    tile = [old_ref[:, 128 * i : 128 * i + 128] for i in range(6)]
    wide = [
        tile[0],
        pltpu.roll(jnp.where(low, tile[2], tile[1]), 64, 1),
        tile[3],
        pltpu.roll(jnp.where(low, tile[5], tile[4]), 64, 1),
    ]
    narrow = [tile[1], pltpu.roll(tile[2], 64, 1), tile[4], pltpu.roll(tile[5], 64, 1)]
    for step, ref in enumerate((own_ref, one_ref, two_ref, three_ref)):
        which = lax.rem(rep + step, 4)
        for start, choice in ((0, wide), (128, [fold(block) for block in narrow])):
            ref[start : start + choice[0].shape[0], :] = jnp.where(
                which == 0,
                choice[0],
                jnp.where(which == 1, choice[1], jnp.where(which == 2, choice[2], choice[3])),
            )


def book_kernel(book_ref, out_ref):
    for g in range(4):
        words = book_ref[:, 8 * g : 8 * g + 8, :].reshape(48, 256)
        norm = jnp.sum((words * words).reshape(6, 8, 256), axis=0)
        first, second, third = (part.astype(F32) for part in split3(-2.0 * words))
        n1, n2, n3 = (part.astype(F32) for part in split3(norm))
        stack = jnp.concatenate([first, second, third, first, second], axis=0)
        for m in range(8):
            mine = jnp.where(iota((240, 256), 0) % 8 == m, stack, 0.0)
            tail_row = iota((16, 256), 0)
            tail = jnp.where(
                tail_row == 0,
                n1[m : m + 1],
                jnp.where(tail_row == 1, n2[m : m + 1], jnp.where(tail_row == 2, n3[m : m + 1], 0.0)),
            )
            out_ref[8 * g + m] = jnp.concatenate([mine, tail], axis=0).T.astype(BF16)


def centroid_kernel(chunk, rep_ref, got_hbm, own_hbm, one_hbm, two_hbm, three_hbm, *refs):
    owners, message = chunk["owners"], chunk["rows"]
    count = len(owners)
    first = chunk["labels"] is not None
    if first:
        back_hbm, cent_hbm, turned_hbm, lab_hbm = refs[:4]
        refs = refs[4:]
    else:
        lab_hbm, _, back_hbm, cent_hbm, turned_hbm = refs[:5]
        refs = refs[5:]
    got_ref, old_ref, back_ref, cent_ref, lab_ref, turned_ref, flip_ref, sem = refs
    rep = rep_ref[0]
    half = 64 * message
    loads = [
        pltpu.make_async_copy(got_hbm.at[pl.ds(half * i, half)], got_ref.at[pl.ds(half * i, half)], sem.at[4 + i])
        for i in range(2)
    ] + [
        pltpu.make_async_copy(src, old_ref.at[i], sem.at[i])
        for i, src in enumerate((own_hbm, one_hbm, two_hbm, three_hbm))
    ]
    if not first:
        loads.append(pltpu.make_async_copy(lab_hbm, lab_ref, sem.at[6]))
    for load in loads:
        load.start()
    if not first:
        loads[6].wait()
    stores = []

    def store(src, dst, at):
        stores.append(pltpu.make_async_copy(src, dst, sem.at[at]))
        stores[-1].start()

    posting = iota((128, 128), 0).astype(F32)
    early = iota((128, 128), 0) % 8 < 4
    spread = (iota((128, 512), 0) == (iota((128, 512), 1) // 128) * 8 + iota((128, 512), 1) % 8).astype(BF16)
    keep = iota((64, 512), 0) % 16 == (iota((64, 512), 1) % 128) // 8
    sums = [None] * count
    counts = [None] * count
    for part in range(2):
        loads[part].wait()
        if first:
            lab = got_ref[pl.ds(half * part + chunk["labels"], 64, stride=message), :].astype(BF16)
            moved = jnp.where(keep, dot(lab, spread), 0.0)
            lab_rows = jnp.sum(moved.reshape(4, 16, 512), axis=1)
            lab_ref[4 * part : 4 * part + 4, :] = lab_rows
        else:
            lab_rows = lab_ref[4 * part : 4 * part + 4, :]
        for c in range(4 * part, 4 * part + 4):
            senders = range(16 * c, 16 * c + 16)
            for members, offset in chunk["narrow"]:
                if len(members) == 2:
                    narrow = jnp.concatenate([got_ref[pl.ds(message * q + offset, 8), :] for q in senders], axis=0)
                else:
                    block = jnp.concatenate(
                        [got_ref[pl.ds(message * q + offset - 4, 8), :] for q in senders], axis=0
                    )
                    narrow = jnp.where(early, pltpu.roll(block, 124, 0), pltpu.roll(block, 64, 1))
                narrow_parts = split2(narrow)
                narrow_turned = narrow.T
                for k, r in enumerate(members):
                    i = r - owners[0]
                    wide = jnp.concatenate([got_ref[pl.ds(message * q + 8 * i, 8), :] for q in senders], axis=0)
                    labels = lab_rows[c - 4 * part : c - 4 * part + 1, 128 * r : 128 * r + 128]
                    hot = (posting == labels).astype(F32)
                    wide_parts = split2(wide)
                    right = jnp.concatenate(
                        [jnp.concatenate([a, b], axis=1) for a, b in zip(wide_parts, narrow_parts)], axis=0
                    )
                    left = hot.astype(BF16)
                    total = dot(jnp.concatenate([left, left], axis=1), right)
                    sums[i] = total if sums[i] is None else sums[i] + total
                    counts[i] = hot if counts[i] is None else counts[i] + hot
                    turned_ref[c, i, 0:128, :] = wide.T
                    turned_ref[c, i, 128:192, :] = narrow_turned[64 * k : 64 * k + 64]
        span = pl.ds(4 * part, 4)
        store(turned_ref.at[span], turned_hbm.at[span], 7 + part)
    for load in loads[2:6]:
        load.wait()
    for members, _ in chunk["narrow"]:
        for k, r in enumerate(members):
            i = r - owners[0]
            step = lax.rem(rep - r + 4, 4)
            weight = prior_weight + jnp.sum(counts[i], axis=1, keepdims=True)
            old = old_ref[step]
            wide = (prior_weight * old[0:128] + sums[i][:, 0:128]) / weight
            tail = sums[i][:, 128:256]
            if k:
                tail = pltpu.roll(tail, 64, 1)
            narrow = (prior_weight * unfold(old[128:192]) + tail) / weight
            back_ref[i, 0:128, :] = wide
            back_ref[i, 128:192, :] = fold(narrow)
            flip_ref[0:128, :] = wide.T
            flip_ref[128:192, :] = narrow.T[0:64]
            for g in range(4):
                for t in range(6):
                    rows = flip_ref[pl.ds(48 * g + t, 8, stride=6), :]
                    for piece, block in enumerate(split2(rows)):
                        at = 48 * piece + 8 * t
                        cent_ref[4 * i + g, at : at + 8, :] = block.astype(F32)
    store(cent_ref, cent_hbm, 9)
    store(back_ref, back_hbm.at[pl.ds(owners[0], count)], 10)
    if first:
        store(lab_ref, lab_hbm, 11)
    for copy in stores:
        copy.wait()


def score_kernel(chunk, turned_hbm, cent_hbm, lab_hbm, book_hbm, *refs):
    if chunk["labels"] is None:
        refs = refs[1:]
    out_hbm, turned_ref, cent2_ref, lab_ref, book_ref, res_ref, norm_ref, out_ref, sem = refs
    owners = chunk["owners"]
    count = len(owners)

    def fetch(src, dst, at):
        return pltpu.make_async_copy(src, dst, sem.at[at])

    def fetch_turned(r):
        return fetch(turned_hbm.at[:, r], turned_ref.at[:, r], r)

    def fetch_book(g):
        return fetch(book_hbm.at[pl.ds(8 * g, 8)], book_ref.at[pl.ds(8 * g, 8)], 4 + g)

    small = [fetch(lab_hbm, lab_ref, 8), fetch(cent_hbm, cent2_ref, 9)]
    for copy in small:
        copy.start()
    fetch_turned(0).start()
    for g in range(4):
        fetch_book(g).start()
    for r in range(1, count):
        fetch_turned(r).start()
    ones = jnp.where(iota((16, 1024), 0) < 3, 1.0, 0.0).astype(BF16)
    res_ref[0, 240:256, :] = ones
    res_ref[1, 240:256, :] = ones
    for copy in small:
        copy.wait()
    fetch_turned(0).wait()

    def prepare(i, buffer):
        r = i // 4
        g = i % 4
        labs = lab_ref[:, pl.ds(pl.multiple_of(128 * (r + owners[0]), 128), 128)]
        posting = iota((128, 128), 0).astype(F32)
        hot = jnp.concatenate([(posting == labs[c : c + 1]).astype(BF16) for c in range(8)], axis=1)
        part = dot(cent2_ref[i].astype(BF16), hot)
        near = part[0:48] + part[48:96]
        rows = jnp.concatenate(
            [
                jnp.concatenate([turned_ref[c, r, pl.ds(48 * g + t, 8, stride=6), :] for c in range(8)], axis=1)
                for t in range(6)
            ],
            axis=0,
        )
        res = rows - near
        norm_ref[buffer] = jnp.sum((res * res).reshape(6, 8, 1024), axis=0)
        first, second = split2(res)
        for spot, piece in enumerate((first, first, first, second, second)):
            res_ref[buffer, 48 * spot : 48 * spot + 48, :] = piece

    def score(i, buffer):
        r = i // 4
        g = i % 4
        right = res_ref[buffer]
        best = []
        for m in range(8):
            value = dot(book_ref[8 * g + m], right)
            value = jnp.min(value.reshape(32, 8, 1024), axis=0)
            best.append(jnp.min(value, axis=0, keepdims=True))
        out_ref[pl.ds(pl.multiple_of(8 * g, 8), 8), pl.ds(pl.multiple_of(1024 * r, 1024), 1024)] = (
            jnp.concatenate(best, axis=0) + norm_ref[buffer]
        )

    prepare(0, 0)

    def step(k, carry):
        @pl.when(k < 4 // 2)
        def _():
            for u in range(2):
                fetch_book(k * 2 + u).wait()

        @pl.when((k % (4 // 2) == 4 // 2 - 1) & (k < 4 * count // 2 - 1))
        def _():
            fetch_turned((k + 1) * 2 // 4).wait()

        for u in range(2):
            i = k * 2 + u
            score(i, u % 2 if 2 > 1 else i % 2)
            prepare(jnp.minimum(i + 1, 4 * count - 1), (u + 1) % 2 if 2 > 1 else (i + 1) % 2)
        return carry

    lax.fori_loop(0, 4 * count // 2, step, 0)
    done = fetch(out_ref, out_hbm.at[:, pl.ds(1024 * owners[0], 1024 * count)], 10)
    done.start()
    done.wait()


def join_kernel(got_ref, out_ref):
    low = iota((128, 128), 1) < 64
    for half in range(2):
        wide0, narrow0 = got_ref[2 * half, 0:128, :], unfold(got_ref[2 * half, 128:192, :])
        wide1, narrow1 = got_ref[2 * half + 1, 0:128, :], unfold(got_ref[2 * half + 1, 128:192, :])
        turned = pltpu.roll(wide1, 64, 1)
        at = 384 * half
        out_ref[:, at : at + 128] = wide0
        out_ref[:, at + 128 : at + 256] = jnp.where(low, narrow0, turned)
        out_ref[:, at + 256 : at + 384] = jnp.where(low, turned, pltpu.roll(narrow1, 64, 1))


def call(kernel, out_shape, specs, out_specs, scratch=(), flops=0, moved=0, limit=LIMIT, aliases=None):
    return pl.pallas_call(
        kernel,
        out_shape=out_shape,
        in_specs=specs,
        out_specs=out_specs,
        scratch_shapes=scratch,
        input_output_aliases=aliases or {},
        compiler_params=pltpu.CompilerParams(vmem_limit_bytes=limit),
        cost_estimate=pl.CostEstimate(flops=flops, bytes_accessed=moved, transcendentals=0),
    )


def shape(*dims, dtype=F32):
    return jax.ShapeDtypeStruct(dims, dtype)


def pack_call(chunk, parts, destination, labels, embeddings):
    message, count = chunk["rows"], len(chunk["owners"])
    return call(
        functools.partial(pack_kernel, chunk, parts),
        shape(128 * message, 128),
        [HBM] * 3,
        HBM,
        [
            pltpu.VMEM((1, 512), jnp.int32),
            pltpu.VMEM((1, 512), jnp.int32),
            pltpu.VMEM((512, 768), F32),
            pltpu.VMEM((128 * message, 128), F32),
            pltpu.VMEM((1024, 768), BF16),
            pltpu.VMEM((2, 256 * count // parts, 768), F32),
            DMA((3 + parts,)),
        ],
        flops=2 * 256 * count * 512 * 768 * 2,
        moved=5 * 2**20,
    )(destination, labels, embeddings)


def exchange(chunk, outgoing):
    message = chunk["rows"]
    return lax.all_to_all(
        outgoing.reshape(128, 1, message * 128), ("shard", "rep"), split_axis=0, concat_axis=0, tiled=True
    ).reshape(128 * message, 128)


def centroid_call(chunk, rep, received, olds, rest):
    message, count = chunk["rows"], len(chunk["owners"])
    first = chunk["labels"] is not None
    outs = [shape(4, 192, 128), shape(4 * count, 96, 128), shape(8, count, 192, 128)]
    if first:
        outs.append(shape(8, 512))
    return call(
        functools.partial(centroid_kernel, chunk),
        outs,
        [SMEM] + [HBM] * (5 + len(rest)),
        [HBM] * len(outs),
        [
            pltpu.VMEM((128 * message, 128), F32),
            pltpu.VMEM((4, 192, 128), F32),
            pltpu.VMEM((count, 192, 128), F32),
            pltpu.VMEM((4 * count, 96, 128), F32),
            pltpu.VMEM((8, 512), F32),
            pltpu.VMEM((8, count, 192, 128), F32),
            pltpu.VMEM((192, 128), F32),
            DMA((12,)),
        ],
        flops=2**28,
        moved=2**23,
        aliases={} if first else {7: 0},
    )(rep, received, *olds, *rest)


def score_call(chunk, turned, cents, lab_rows, book, rest):
    count = len(chunk["owners"])
    return call(
        functools.partial(score_kernel, chunk),
        shape(32, 4096),
        [HBM] * (4 + len(rest)),
        HBM,
        [
            pltpu.VMEM((8, count, 192, 128), F32),
            pltpu.VMEM((4 * count, 96, 128), F32),
            pltpu.VMEM((8, 512), F32),
            pltpu.VMEM((32, 256, 256), BF16),
            pltpu.VMEM((2, 256, 1024), BF16),
            pltpu.VMEM((2, 8, 1024), F32),
            pltpu.VMEM((32, 1024 * count), F32),
            DMA((11,)),
        ],
        flops=2**28,
        moved=2**23,
        aliases={4: 0} if rest else {},
    )(turned, cents, lab_rows, book, *rest)


def local(embeddings, destination, labels, old_centroids, codebook):
    rep = lax.axis_index("rep").astype(jnp.int32).reshape(1)
    destination, labels = destination.reshape(1, 512), labels.reshape(1, 512)
    outgoing = pack_call(ALL, 4, destination, labels, embeddings)
    quarters = call(
        quarters_kernel, [shape(192, 128)] * 4, [SMEM, VMEM], [VMEM] * 4, flops=2**20, moved=2**20
    )(rep, old_centroids)
    olds = [quarters[0]]
    for step in (1, 2, 3):
        olds.append(lax.ppermute(quarters[step], "rep", [(i, (i + step) % 4) for i in range(4)]))
    book = call(
        book_kernel, shape(32, 256, 256, dtype=BF16), [VMEM], VMEM, flops=2**28, moved=5 * 2**20
    )(jnp.transpose(codebook, (2, 0, 1)))

    received = exchange(ALL, outgoing)
    received, book = lax.optimization_barrier((received, book))
    back, cents, turned, lab_rows = centroid_call(ALL, rep, received, olds, ())
    returned = lax.all_to_all(back, "rep", split_axis=0, concat_axis=0, tiled=True)
    scores = score_call(ALL, turned, cents, lab_rows, book, ())
    centroids = call(join_kernel, shape(128, 768), [VMEM], VMEM, flops=2**18, moved=2**20, limit=16 * 2**20)(returned)
    return (centroids, scores)


def solution(mesh):
    placed = (
        P(("shard", "rep"), None),
        P(("shard", "rep"), None),
        P(("shard", "rep")),
        P(("shard", "rep"), None),
        P("rep", None, None),
    )
    return jax.shard_map(
        local,
        mesh=mesh,
        in_specs=placed,
        out_specs=(P(("shard", "rep"), None), P("rep", "shard")),
        check_vma=False,
    )
```

```python
import functools
import jax
import jax.numpy as jnp
from jax import lax
from jax.experimental import pallas as pl
from jax.experimental.pallas import tpu as pltpu
from jax.sharding import PartitionSpec as P

prior_weight = 8.0
F32 = jnp.float32
BF16 = jnp.bfloat16
VMEM = pl.BlockSpec(memory_space=pltpu.VMEM)
SMEM = pl.BlockSpec(memory_space=pltpu.SMEM)
HBM = pl.BlockSpec(memory_space=pltpu.HBM)
DMA = pltpu.SemaphoreType.DMA
LIMIT = 58 * 2**20
SUMS_LIMIT = 24 * 2**20

ALL = {"owners": (0, 1, 2, 3), "narrow": (((0, 1), 33), ((2, 3), 41)), "labels": 0, "wide": 1, "rows": 49}


def split2(x):
    first = x.astype(BF16)
    return first, (x - first.astype(F32)).astype(BF16)


def split3(x):
    first, second = split2(x)
    third = (x - first.astype(F32) - second.astype(F32)).astype(BF16)
    return first, second, third


def iota(shape, dim):
    return lax.broadcasted_iota(jnp.int32, shape, dim)


def dot(a, b):
    return jnp.dot(a, b, preferred_element_type=F32)


def pack_kernel(
    chunk, parts, dest_hbm, label_hbm, rows_hbm, out_hbm, dest_ref, label_ref, rows_ref, out_ref, a_ref, b_ref, sem
):
    owners, message = chunk["owners"], chunk["rows"]
    count = len(owners)
    loads = [
        pltpu.make_async_copy(src, dst, sem.at[i])
        for i, (src, dst) in enumerate(((dest_hbm, dest_ref), (label_hbm, label_ref), (rows_hbm, rows_ref)))
    ]
    for load in loads:
        load.start()
    loads[0].wait()
    dest = dest_ref[...]
    named = (iota((128, 512), 0) == dest).astype(F32)
    earlier = (iota((512, 512), 0) < iota((512, 512), 1)).astype(BF16)
    before = dot(named.astype(BF16), earlier)
    spot = jnp.sum(named * before, axis=0, keepdims=True).astype(jnp.int32)
    shard, owner = dest // 4, dest % 4
    place = (owner - owners[0]) * 8 + spot
    chosen = (owner >= owners[0]) & (owner <= owners[-1])
    slot = jnp.where(chosen, shard * (8 * count) + place, -1)

    loads[1].wait()
    if chunk["labels"] is not None:
        group = (iota((32, 512), 0) == shard).astype(F32)
        within = (iota((128, 512), 0) == owner * 8 + spot).astype(BF16)
        labels = group * (label_ref[...] + 1).astype(F32)
        label_rows = lax.dot_general(
            labels.astype(BF16), within, (((1,), (1,)), ((), ())), preferred_element_type=F32
        ) - 1.0
        for quarter in range(4):
            out_ref[pl.ds(message * quarter + chunk["labels"], 32, stride=4 * message), :] = label_rows

    loads[2].wait()
    low = iota((512, 128), 1) < 64
    tile = [rows_ref[:, 128 * i : 128 * i + 128] for i in range(6)]
    wide = [
        tile[0],
        pltpu.roll(jnp.where(low, tile[2], tile[1]), 64, 1),
        tile[3],
        pltpu.roll(jnp.where(low, tile[5], tile[4]), 64, 1),
    ]
    narrow = [jnp.where(low, tile[1], tile[2]), jnp.where(low, tile[4], tile[5])]
    for i, block in enumerate(wide + narrow):
        for piece, part in enumerate(split2(block)):
            a_ref[512 * piece : 512 * piece + 512, 128 * i : 128 * i + 128] = part

    lower = iota((8, 128), 1) < 64
    stores = []
    groups = 32 // parts
    for part in range(parts):
        size = groups * 8 * count
        pick = (iota((size, 512), 0) + size * part == slot).astype(BF16)
        got = b_ref.at[part % 2]
        got[...] = dot(pick, a_ref[0:512, :]) + dot(pick, a_ref[512:1024, :])
        for s in range(groups):
            for quarter in range(4):
                base = message * (4 * (groups * part + s) + quarter)
                at = 8 * count * s
                out_ref[pl.ds(base + chunk["wide"], 8 * count), :] = got[at : at + 8 * count, 128 * quarter : 128 * quarter + 128]
                lanes = 512 + 128 * (quarter // 2)
                for members, offset in chunk["narrow"]:
                    rows = [at + 8 * (r - owners[0]) for r in members]
                    one = got[rows[0] : rows[0] + 8, lanes : lanes + 128]
                    two = got[rows[1] : rows[1] + 8, lanes : lanes + 128]
                    if quarter % 2 == 0:
                        both = jnp.where(lower, one, pltpu.roll(two, 64, 1))
                    else:
                        both = jnp.where(lower, pltpu.roll(one, 64, 1), two)
                    out_ref[pl.ds(base + offset, 8), :] = both
        span = pl.ds(128 * message // parts * part, 128 * message // parts)
        stores.append(pltpu.make_async_copy(out_ref.at[span], out_hbm.at[span], sem.at[3 + part]))
        stores[-1].start()
    for store in stores:
        store.wait()


def fold(block):
    return jnp.where(iota((64, 128), 1) < 64, block[0:64], pltpu.roll(block[64:128], 64, 1))


def unfold(block):
    return jnp.concatenate([block, pltpu.roll(block, 64, 1)], axis=0)


def quarters_kernel(rep_ref, old_ref, own_ref, one_ref, two_ref, three_ref):
    rep = rep_ref[0]
    low = iota((128, 128), 1) < 64
    tile = [old_ref[:, 128 * i : 128 * i + 128] for i in range(6)]
    wide = [
        tile[0],
        pltpu.roll(jnp.where(low, tile[2], tile[1]), 64, 1),
        tile[3],
        pltpu.roll(jnp.where(low, tile[5], tile[4]), 64, 1),
    ]
    narrow = [tile[1], pltpu.roll(tile[2], 64, 1), tile[4], pltpu.roll(tile[5], 64, 1)]
    for step, ref in enumerate((own_ref, one_ref, two_ref, three_ref)):
        which = lax.rem(rep + step, 4)
        for start, choice in ((0, wide), (128, [fold(block) for block in narrow])):
            ref[start : start + choice[0].shape[0], :] = jnp.where(
                which == 0,
                choice[0],
                jnp.where(which == 1, choice[1], jnp.where(which == 2, choice[2], choice[3])),
            )


def book_kernel(book_ref, out_ref):
    for g in range(4):
        words = book_ref[:, 8 * g : 8 * g + 8, :].reshape(48, 256)
        norm = jnp.sum((words * words).reshape(6, 8, 256), axis=0)
        first, second, third = (part.astype(F32) for part in split3(-2.0 * words))
        n1, n2, n3 = (part.astype(F32) for part in split3(norm))
        stack = jnp.concatenate([first, second, third, first, second], axis=0)
        for m in range(8):
            mine = jnp.where(iota((240, 256), 0) % 8 == m, stack, 0.0)
            tail_row = iota((16, 256), 0)
            tail = jnp.where(
                tail_row == 0,
                n1[m : m + 1],
                jnp.where(tail_row == 1, n2[m : m + 1], jnp.where(tail_row == 2, n3[m : m + 1], 0.0)),
            )
            out_ref[8 * g + m] = jnp.concatenate([mine, tail], axis=0).T.astype(BF16)


def label_rows(got_ref):
    spread = (iota((128, 512), 0) == (iota((128, 512), 1) // 128) * 8 + iota((128, 512), 1) % 8).astype(BF16)
    keep = iota((128, 512), 0) % 16 == (iota((128, 512), 1) % 128) // 8
    lab = got_ref[pl.ds(ALL["labels"], 128, stride=ALL["rows"]), :].astype(BF16)
    return jnp.sum(jnp.where(keep, dot(lab, spread), 0.0).reshape(8, 16, 512), axis=1)


def tile_rows(got_ref, c, offset):
    return jnp.concatenate([got_ref[pl.ds(ALL["rows"] * q + offset, 8), :] for q in range(16 * c, 16 * c + 16)], axis=0)


def sums_kernel(got_ref, sums_ref):
    posting = iota((128, 128), 0).astype(F32)
    lab = label_rows(got_ref)
    sums = [None] * 4
    counts = [None] * 4
    for c in range(8):
        for members, offset in ALL["narrow"]:
            narrow_parts = split2(tile_rows(got_ref, c, offset))
            for r in members:
                hot = (posting == lab[c : c + 1, 128 * r : 128 * r + 128]).astype(F32)
                right = jnp.concatenate(
                    [
                        jnp.concatenate([a, b], axis=1)
                        for a, b in zip(split2(tile_rows(got_ref, c, ALL["wide"] + 8 * r)), narrow_parts)
                    ],
                    axis=0,
                )
                left = hot.astype(BF16)
                total = dot(jnp.concatenate([left, left], axis=1), right)
                sums[r] = total if sums[r] is None else sums[r] + total
                counts[r] = hot if counts[r] is None else counts[r] + hot
    for members, _ in ALL["narrow"]:
        for k, r in enumerate(members):
            tail = sums[r][:, 128:256]
            if k:
                tail = pltpu.roll(tail, 64, 1)
            sums_ref[r, 0:128, :] = sums[r][:, 0:128]
            sums_ref[r, 128:192, :] = fold(tail)
            sums_ref[r, 192:200, :] = jnp.broadcast_to(jnp.sum(counts[r].T, axis=0, keepdims=True), (8, 128))


def score_kernel(
    rep_ref, got_hbm, sums_hbm, book_hbm, own_hbm, one_hbm, two_hbm, three_hbm, out_hbm,
    got_ref, work_ref, lab_ref, sums_ref, book_ref, old_ref, flip_ref, cent_ref, piece_ref, norm_ref, out_ref, sem,
):
    def fetch(src, dst, at):
        return pltpu.make_async_copy(src, dst, sem.at[at])

    def fetch_book(g):
        return fetch(book_hbm.at[pl.ds(8 * g, 8)], book_ref.at[pl.ds(8 * g, 8)], 4 + g)

    def send(r):
        span = pl.ds(pl.multiple_of(1024 * r, 1024), 1024)
        return fetch(out_ref.at[r], out_hbm.at[:, span], 14 + r)

    rows = []
    for i in range(4):
        span = pl.ds(32 * ALL["rows"] * i, 32 * ALL["rows"])
        rows.append(fetch(got_hbm.at[span], got_ref.at[span], 18 + i))
        rows[i].start()
    small = [fetch(sums_hbm, sums_ref, 8)]
    small += [fetch(src, old_ref.at[i], 10 + i) for i, src in enumerate((own_hbm, one_hbm, two_hbm, three_hbm))]
    for copy in small:
        copy.start()
    for g in range(4):
        fetch_book(g).start()
    rep = rep_ref[0]
    for c in range(8):
        if c % 2 == 0:
            rows[c // 2].wait()
        for members, offset in ALL["narrow"]:
            narrow = tile_rows(got_ref, c, offset).T
            for k, r in enumerate(members):
                at = 192 * (8 * r + c)
                work_ref[at : at + 128, :] = tile_rows(got_ref, c, ALL["wide"] + 8 * r).T
                work_ref[at + 128 : at + 192, :] = narrow[64 * k : 64 * k + 64]
    lab = label_rows(got_ref)
    for copy in small:
        copy.wait()
    for r in range(4):
        lab_ref[r] = lab[:, 128 * r : 128 * r + 128]
        total = prior_weight * old_ref[lax.rem(rep - r + 4, 4)] + sums_ref[r, 0:192, :]
        weight = prior_weight + sums_ref[r, 192:193, :]
        flip_ref[0:128, :] = total[0:128].T / weight
        flip_ref[128:192, :] = unfold(total[128:192]).T[0:64] / weight
        for g in range(4):
            for t in range(6):
                for piece, block in enumerate(split2(flip_ref[pl.ds(48 * g + t, 8, stride=6), :])):
                    at = 192 * piece + 48 * g + 8 * t
                    cent_ref[r, at : at + 8, :] = block.astype(F32)

    def prepare(r, buffer):
        labs = lab_ref[r]
        posting = iota((128, 128), 0).astype(F32)
        hot = jnp.concatenate([(posting == labs[c : c + 1]).astype(BF16) for c in range(8)], axis=1)
        near = dot(cent_ref[r].astype(BF16), hot)
        for g in range(4):
            span = slice(48 * g, 48 * g + 48)
            rows = jnp.concatenate(
                [
                    jnp.concatenate(
                        [work_ref[pl.ds(192 * (8 * r + c) + 48 * g + t, 8, stride=6), :] for c in range(8)], axis=1
                    )
                    for t in range(6)
                ],
                axis=0,
            )
            res = rows - (near[span] + near[192 + 48 * g : 240 + 48 * g])
            norm_ref[buffer, 8 * g : 8 * g + 8, :] = jnp.sum((res * res).reshape(6, 8, 1024), axis=0)
            for i, piece in enumerate(split2(res)):
                piece_ref[buffer, i, span, :] = piece

    ones = jnp.where(iota((16, 1024), 0) < 3, 1.0, 0.0).astype(BF16)

    def score(r, g, buffer):
        first = piece_ref[buffer, 0, 48 * g : 48 * g + 48, :]
        second = piece_ref[buffer, 1, 48 * g : 48 * g + 48, :]
        right = jnp.concatenate([first, first, first, second, second, ones], axis=0)
        best = []
        for m in range(8):
            value = dot(book_ref[8 * g + m], right)
            value = jnp.min(value.reshape(32, 8, 1024), axis=0)
            best.append(jnp.min(value, axis=0, keepdims=True))
        out_ref[r, 8 * g : 8 * g + 8, :] = jnp.concatenate(best, axis=0) + norm_ref[buffer, 8 * g : 8 * g + 8, :]

    prepare(0, 0)
    for g in range(4):
        fetch_book(g).wait()

    def step(r, carry):
        for g in range(4):
            score(r, g, r % 2)
        prepare(jnp.minimum(r + 1, 3), (r + 1) % 2)
        send(r).start()
        return carry

    lax.fori_loop(0, 4, step, 0)
    for r in range(4):
        send(r).wait()


def join_kernel(got_hbm, old_hbm, out_hbm, got_ref, old_ref, out_ref, sem):
    loads = [
        pltpu.make_async_copy(src, dst, sem.at[i]) for i, (src, dst) in enumerate(((got_hbm, got_ref), (old_hbm, old_ref)))
    ]
    for load in loads:
        load.start()
    for load in loads:
        load.wait()
    weight = prior_weight + jnp.broadcast_to(got_ref[0, 192:193, :], (128, 128)).T
    low = iota((128, 128), 1) < 64
    for half in range(2):
        wide0, narrow0 = got_ref[2 * half, 0:128, :], unfold(got_ref[2 * half, 128:192, :])
        wide1, narrow1 = got_ref[2 * half + 1, 0:128, :], unfold(got_ref[2 * half + 1, 128:192, :])
        turned = pltpu.roll(wide1, 64, 1)
        sums = (wide0, jnp.where(low, narrow0, turned), jnp.where(low, turned, pltpu.roll(narrow1, 64, 1)))
        for i in range(3):
            at = 384 * half + 128 * i
            out_ref[:, at : at + 128] = (prior_weight * old_ref[:, at : at + 128] + sums[i]) / weight
    store = pltpu.make_async_copy(out_ref, out_hbm, sem.at[2])
    store.start()
    store.wait()


def call(kernel, out_shape, specs, out_specs, scratch=(), flops=0, moved=0, limit=LIMIT):
    return pl.pallas_call(
        kernel,
        out_shape=out_shape,
        in_specs=specs,
        out_specs=out_specs,
        scratch_shapes=scratch,
        compiler_params=pltpu.CompilerParams(vmem_limit_bytes=limit),
        cost_estimate=pl.CostEstimate(flops=flops, bytes_accessed=moved, transcendentals=0),
    )


def shape(*dims, dtype=F32):
    return jax.ShapeDtypeStruct(dims, dtype)


def pack_call(chunk, parts, destination, labels, embeddings):
    message, count = chunk["rows"], len(chunk["owners"])
    return call(
        functools.partial(pack_kernel, chunk, parts),
        shape(128 * message, 128),
        [HBM] * 3,
        HBM,
        [
            pltpu.VMEM((1, 512), jnp.int32),
            pltpu.VMEM((1, 512), jnp.int32),
            pltpu.VMEM((512, 768), F32),
            pltpu.VMEM((132 * message, 128), F32),
            pltpu.VMEM((1024, 768), BF16),
            pltpu.VMEM((2, 256 * count // parts, 768), F32),
            DMA((3 + parts,)),
        ],
        flops=2 * 256 * count * 512 * 768 * 2,
        moved=5 * 2**20,
    )(destination, labels, embeddings)


def exchange(chunk, outgoing):
    message = chunk["rows"]
    return lax.all_to_all(
        outgoing.reshape(128, 1, message * 128), ("shard", "rep"), split_axis=0, concat_axis=0, tiled=True
    ).reshape(128 * message, 128)


def score_call(rep, received, sums, book, olds):
    return call(
        score_kernel,
        shape(32, 4096),
        [SMEM] + [HBM] * 7,
        HBM,
        [
            pltpu.VMEM((128 * ALL["rows"], 128), F32),
            pltpu.VMEM((6160, 128), F32),
            pltpu.VMEM((4, 8, 128), F32),
            pltpu.VMEM((4, 200, 128), F32),
            pltpu.VMEM((32, 256, 256), BF16),
            pltpu.VMEM((4, 192, 128), F32),
            pltpu.VMEM((208, 128), F32),
            pltpu.VMEM((4, 384, 128), F32),
            pltpu.VMEM((2, 2, 192, 1024), BF16),
            pltpu.VMEM((2, 32, 1024), F32),
            pltpu.VMEM((4, 32, 1024), F32),
            DMA((22,)),
        ],
        flops=2**32,
        moved=2**23,
    )(rep, received, sums, book, *olds)


def local(embeddings, destination, labels, old_centroids, codebook):
    rep = lax.axis_index("rep").astype(jnp.int32).reshape(1)
    destination, labels = destination.reshape(1, 512), labels.reshape(1, 512)
    outgoing = pack_call(ALL, 4, destination, labels, embeddings)
    book = call(
        book_kernel, shape(32, 256, 256, dtype=BF16), [VMEM], VMEM, flops=2**28, moved=5 * 2**20
    )(jnp.transpose(codebook, (2, 0, 1)))

    old_centroids, book = lax.optimization_barrier((old_centroids, book))
    quarters = call(
        quarters_kernel, [shape(192, 128)] * 4, [SMEM, VMEM], [VMEM] * 4, flops=2**20, moved=2**20
    )(rep, old_centroids)
    olds = [quarters[0]]
    for step in (1, 2, 3):
        olds.append(lax.ppermute(quarters[step], "rep", [(i, (i + step) % 4) for i in range(4)]))

    received = exchange(ALL, outgoing)
    received, book = lax.optimization_barrier((received, book))
    sums = call(
        sums_kernel, shape(4, 200, 128), [VMEM], VMEM, flops=2**28, moved=2**22, limit=SUMS_LIMIT
    )(received)
    returned = lax.all_to_all(sums, "rep", split_axis=0, concat_axis=0, tiled=True)
    scores = score_call(rep, received, sums, book, olds)
    centroids = call(
        join_kernel,
        shape(128, 768),
        [HBM] * 2,
        HBM,
        [pltpu.VMEM((4, 200, 128), F32), pltpu.VMEM((128, 768), F32), pltpu.VMEM((128, 768), F32), DMA((3,))],
        flops=2**18,
        moved=2**20,
    )(returned, old_centroids)
    return (centroids, scores)


def solution(mesh):
    placed = (
        P(("shard", "rep"), None),
        P(("shard", "rep"), None),
        P(("shard", "rep")),
        P(("shard", "rep"), None),
        P("rep", None, None),
    )
    return jax.shard_map(
        local,
        mesh=mesh,
        in_specs=placed,
        out_specs=(P(("shard", "rep"), None), P("rep", "shard")),
        check_vma=False,
    )
```

```python
import functools
import jax
import jax.numpy as jnp
from jax import lax
from jax.experimental import pallas as pl
from jax.experimental.pallas import tpu as pltpu
from jax.sharding import PartitionSpec as P

prior_weight = 8.0
F32 = jnp.float32
BF16 = jnp.bfloat16
VMEM = pl.BlockSpec(memory_space=pltpu.VMEM)
SMEM = pl.BlockSpec(memory_space=pltpu.SMEM)
HBM = pl.BlockSpec(memory_space=pltpu.HBM)
DMA = pltpu.SemaphoreType.DMA
LIMIT = 58 * 2**20
SUMS_LIMIT = 24 * 2**20
SCORE_LIMIT = 51 * 2**20
JOIN_LIMIT = 16 * 2**20

ALL = {"owners": (0, 1, 2, 3), "narrow": (((0, 1), 33), ((2, 3), 41)), "labels": 0, "wide": 1, "rows": 49}


def split2(x):
    first = x.astype(BF16)
    return first, (x - first.astype(F32)).astype(BF16)


def split3(x):
    first, second = split2(x)
    third = (x - first.astype(F32) - second.astype(F32)).astype(BF16)
    return first, second, third


def iota(shape, dim):
    return lax.broadcasted_iota(jnp.int32, shape, dim)


def dot(a, b):
    return jnp.dot(a, b, preferred_element_type=F32)


def pack_kernel(
    chunk, parts, dest_hbm, label_hbm, rows_hbm, out_hbm, dest_ref, label_ref, rows_ref, out_ref, a_ref, b_ref, sem
):
    owners, message = chunk["owners"], chunk["rows"]
    count = len(owners)
    loads = [
        pltpu.make_async_copy(src, dst, sem.at[i])
        for i, (src, dst) in enumerate(((dest_hbm, dest_ref), (label_hbm, label_ref), (rows_hbm, rows_ref)))
    ]
    for load in loads:
        load.start()
    loads[0].wait()
    dest = dest_ref[...]
    named = (iota((128, 512), 0) == dest).astype(F32)
    earlier = (iota((512, 512), 0) < iota((512, 512), 1)).astype(BF16)
    before = dot(named.astype(BF16), earlier)
    spot = jnp.sum(named * before, axis=0, keepdims=True).astype(jnp.int32)
    shard, owner = dest // 4, dest % 4
    place = (owner - owners[0]) * 8 + spot
    chosen = (owner >= owners[0]) & (owner <= owners[-1])
    slot = jnp.where(chosen, shard * (8 * count) + place, -1)

    loads[1].wait()
    if chunk["labels"] is not None:
        group = (iota((32, 512), 0) == shard).astype(F32)
        within = (iota((128, 512), 0) == owner * 8 + spot).astype(BF16)
        labels = group * (label_ref[...] + 1).astype(F32)
        label_rows = lax.dot_general(
            labels.astype(BF16), within, (((1,), (1,)), ((), ())), preferred_element_type=F32
        ) - 1.0
        for quarter in range(4):
            out_ref[pl.ds(message * quarter + chunk["labels"], 32, stride=4 * message), :] = label_rows

    loads[2].wait()
    low = iota((512, 128), 1) < 64
    tile = [rows_ref[:, 128 * i : 128 * i + 128] for i in range(6)]
    wide = [
        tile[0],
        pltpu.roll(jnp.where(low, tile[2], tile[1]), 64, 1),
        tile[3],
        pltpu.roll(jnp.where(low, tile[5], tile[4]), 64, 1),
    ]
    narrow = [jnp.where(low, tile[1], tile[2]), jnp.where(low, tile[4], tile[5])]
    for i, block in enumerate(wide + narrow):
        for piece, part in enumerate(split2(block)):
            a_ref[512 * piece : 512 * piece + 512, 128 * i : 128 * i + 128] = part

    lower = iota((8, 128), 1) < 64
    stores = []
    groups = 32 // parts
    for part in range(parts):
        size = groups * 8 * count
        pick = (iota((size, 512), 0) + size * part == slot).astype(BF16)
        got = b_ref.at[part % 2]
        got[...] = dot(pick, a_ref[0:512, :]) + dot(pick, a_ref[512:1024, :])
        for s in range(groups):
            for quarter in range(4):
                base = message * (4 * (groups * part + s) + quarter)
                at = 8 * count * s
                out_ref[pl.ds(base + chunk["wide"], 8 * count), :] = got[at : at + 8 * count, 128 * quarter : 128 * quarter + 128]
                lanes = 512 + 128 * (quarter // 2)
                for members, offset in chunk["narrow"]:
                    rows = [at + 8 * (r - owners[0]) for r in members]
                    one = got[rows[0] : rows[0] + 8, lanes : lanes + 128]
                    two = got[rows[1] : rows[1] + 8, lanes : lanes + 128]
                    if quarter % 2 == 0:
                        both = jnp.where(lower, one, pltpu.roll(two, 64, 1))
                    else:
                        both = jnp.where(lower, pltpu.roll(one, 64, 1), two)
                    out_ref[pl.ds(base + offset, 8), :] = both
        span = pl.ds(128 * message // parts * part, 128 * message // parts)
        stores.append(pltpu.make_async_copy(out_ref.at[span], out_hbm.at[span], sem.at[3 + part]))
        stores[-1].start()
    for store in stores:
        store.wait()


def fold(block):
    return jnp.where(iota((64, 128), 1) < 64, block[0:64], pltpu.roll(block[64:128], 64, 1))


def unfold(block):
    return jnp.concatenate([block, pltpu.roll(block, 64, 1)], axis=0)


def quarters_kernel(rep_ref, old_ref, own_ref, one_ref, two_ref, three_ref):
    rep = rep_ref[0]
    low = iota((128, 128), 1) < 64
    tile = [old_ref[:, 128 * i : 128 * i + 128] for i in range(6)]
    wide = [
        tile[0],
        pltpu.roll(jnp.where(low, tile[2], tile[1]), 64, 1),
        tile[3],
        pltpu.roll(jnp.where(low, tile[5], tile[4]), 64, 1),
    ]
    narrow = [tile[1], pltpu.roll(tile[2], 64, 1), tile[4], pltpu.roll(tile[5], 64, 1)]
    for step, ref in enumerate((own_ref, one_ref, two_ref, three_ref)):
        which = lax.rem(rep + step, 4)
        for start, choice in ((0, wide), (128, [fold(block) for block in narrow])):
            ref[start : start + choice[0].shape[0], :] = jnp.where(
                which == 0,
                choice[0],
                jnp.where(which == 1, choice[1], jnp.where(which == 2, choice[2], choice[3])),
            )


def book_kernel(book_ref, out_ref):
    for g in range(4):
        words = book_ref[:, 8 * g : 8 * g + 8, :].reshape(48, 256)
        norm = jnp.sum((words * words).reshape(6, 8, 256), axis=0)
        first, second, third = (part.astype(F32) for part in split3(-2.0 * words))
        n1, n2, n3 = (part.astype(F32) for part in split3(norm))
        stack = jnp.concatenate([first, second, third, first, second], axis=0)
        for m in range(8):
            mine = jnp.where(iota((240, 256), 0) % 8 == m, stack, 0.0)
            tail_row = iota((16, 256), 0)
            tail = jnp.where(
                tail_row == 0,
                n1[m : m + 1],
                jnp.where(tail_row == 1, n2[m : m + 1], jnp.where(tail_row == 2, n3[m : m + 1], 0.0)),
            )
            out_ref[8 * g + m] = jnp.concatenate([mine, tail], axis=0).T.astype(BF16)


def label_rows(got_ref):
    spread = (iota((128, 512), 0) == (iota((128, 512), 1) // 128) * 8 + iota((128, 512), 1) % 8).astype(BF16)
    keep = iota((128, 512), 0) % 16 == (iota((128, 512), 1) % 128) // 8
    lab = got_ref[pl.ds(ALL["labels"], 128, stride=ALL["rows"]), :].astype(BF16)
    return jnp.sum(jnp.where(keep, dot(lab, spread), 0.0).reshape(8, 16, 512), axis=1)


def tile_rows(got_ref, c, offset):
    return jnp.concatenate([got_ref[pl.ds(ALL["rows"] * q + offset, 8), :] for q in range(16 * c, 16 * c + 16)], axis=0)


def sums_kernel(rep_ref, got_ref, sums_ref, one_ref, two_ref, three_ref):
    posting = iota((128, 128), 0).astype(F32)
    lab = label_rows(got_ref)
    sums = [None] * 4
    counts = [None] * 4
    for c in range(8):
        for members, offset in ALL["narrow"]:
            narrow_parts = split2(tile_rows(got_ref, c, offset))
            for r in members:
                hot = (posting == lab[c : c + 1, 128 * r : 128 * r + 128]).astype(F32)
                right = jnp.concatenate(
                    [
                        jnp.concatenate([a, b], axis=1)
                        for a, b in zip(split2(tile_rows(got_ref, c, ALL["wide"] + 8 * r)), narrow_parts)
                    ],
                    axis=0,
                )
                left = hot.astype(BF16)
                total = dot(jnp.concatenate([left, left], axis=1), right)
                sums[r] = total if sums[r] is None else sums[r] + total
                counts[r] = hot if counts[r] is None else counts[r] + hot
    for members, _ in ALL["narrow"]:
        for k, r in enumerate(members):
            tail = sums[r][:, 128:256]
            if k:
                tail = pltpu.roll(tail, 64, 1)
            sums_ref[r, 0:128, :] = sums[r][:, 0:128]
            sums_ref[r, 128:192, :] = fold(tail)
            sums_ref[r, 192:200, :] = jnp.broadcast_to(jnp.sum(counts[r].T, axis=0, keepdims=True), (8, 128))
    for step, ref in ((1, one_ref), (2, two_ref), (3, three_ref)):
        ref[...] = sums_ref[lax.rem(rep_ref[0] + step, 4)]


def score_kernel(
    rep_ref, got_hbm, sums_hbm, book_hbm, own_hbm, one_hbm, two_hbm, three_hbm, out_hbm,
    got_ref, work_ref, lab_ref, sums_ref, book_ref, old_ref, flip_ref, cent_ref, piece_ref, norm_ref, out_ref, sem,
):
    def fetch(src, dst, at):
        return pltpu.make_async_copy(src, dst, sem.at[at])

    def fetch_book(g):
        return fetch(book_hbm.at[pl.ds(8 * g, 8)], book_ref.at[pl.ds(8 * g, 8)], 4 + g)

    def send(r):
        span = pl.ds(pl.multiple_of(1024 * r, 1024), 1024)
        return fetch(out_ref.at[r], out_hbm.at[:, span], 14 + r)

    rows = []
    for i in range(4):
        span = pl.ds(32 * ALL["rows"] * i, 32 * ALL["rows"])
        rows.append(fetch(got_hbm.at[span], got_ref.at[span], 18 + i))
        rows[i].start()
    small = [fetch(sums_hbm, sums_ref, 8)]
    small += [fetch(src, old_ref.at[i], 10 + i) for i, src in enumerate((own_hbm, one_hbm, two_hbm, three_hbm))]
    for copy in small:
        copy.start()
    for g in range(4):
        fetch_book(g).start()
    rep = rep_ref[0]
    for c in range(8):
        if c % 2 == 0:
            rows[c // 2].wait()
        for members, offset in ALL["narrow"]:
            narrow = tile_rows(got_ref, c, offset).T
            for k, r in enumerate(members):
                at = 192 * (8 * r + c)
                work_ref[at : at + 128, :] = tile_rows(got_ref, c, ALL["wide"] + 8 * r).T
                work_ref[at + 128 : at + 192, :] = narrow[64 * k : 64 * k + 64]
    lab = label_rows(got_ref)
    for copy in small:
        copy.wait()
    for r in range(4):
        lab_ref[r] = lab[:, 128 * r : 128 * r + 128]
        total = prior_weight * old_ref[lax.rem(rep - r + 4, 4)] + sums_ref[r, 0:192, :]
        weight = prior_weight + sums_ref[r, 192:193, :]
        flip_ref[0:128, :] = total[0:128].T / weight
        flip_ref[128:192, :] = unfold(total[128:192]).T[0:64] / weight
        for g in range(4):
            for t in range(6):
                for piece, block in enumerate(split2(flip_ref[pl.ds(48 * g + t, 8, stride=6), :])):
                    at = 192 * piece + 48 * g + 8 * t
                    cent_ref[r, at : at + 8, :] = block.astype(F32)

    def prepare(r, half, buffer):
        labs = lab_ref[r]
        lanes = slice(1024 * half, 1024 * half + 1024)
        posting = iota((128, 128), 0).astype(F32)
        hot = jnp.concatenate([(posting == labs[c : c + 1]).astype(BF16) for c in range(8)], axis=1)
        near = dot(cent_ref[r].astype(BF16), hot)
        for g in range(4):
            span = slice(48 * g, 48 * g + 48)
            rows = jnp.concatenate(
                [
                    jnp.concatenate(
                        [work_ref[pl.ds(192 * (8 * r + c) + 48 * g + t, 8, stride=6), :] for c in range(8)], axis=1
                    )
                    for t in range(6)
                ],
                axis=0,
            )
            res = rows - (near[span] + near[192 + 48 * g : 240 + 48 * g])
            norm_ref[buffer, 8 * g : 8 * g + 8, lanes] = jnp.sum((res * res).reshape(6, 8, 1024), axis=0)
            for i, piece in enumerate(split2(res)):
                piece_ref[buffer, i, span, lanes] = piece

    ones = jnp.where(iota((16, 2048), 0) < 3, 1.0, 0.0).astype(BF16)

    def score(r, g, buffer):
        first = piece_ref[buffer, 0, 48 * g : 48 * g + 48, :]
        second = piece_ref[buffer, 1, 48 * g : 48 * g + 48, :]
        right = jnp.concatenate([first, first, first, second, second, ones], axis=0)
        best = []
        for m in range(8):
            value = dot(book_ref[8 * g + m], right)
            value = jnp.min(value.reshape(32, 8, 2048), axis=0)
            best.append(jnp.min(value, axis=0, keepdims=True))
        result = jnp.concatenate(best, axis=0) + norm_ref[buffer, 8 * g : 8 * g + 8, :]
        out_ref[r, 8 * g : 8 * g + 8, :] = result[:, 0:1024]
        out_ref[r + 1, 8 * g : 8 * g + 8, :] = result[:, 1024:2048]

    prepare(0, 0, 0)
    prepare(1, 1, 0)
    for g in range(4):
        fetch_book(g).wait()
    for pair in range(2):
        for g in range(4):
            score(2 * pair, g, pair)
        if pair == 0:
            prepare(2, 0, 1)
            prepare(3, 1, 1)
        send(2 * pair).start()
        send(2 * pair + 1).start()
    for r in range(4):
        send(r).wait()


def join_kernel(
    rep_ref, own_hbm, one_hbm, two_hbm, three_hbm, old_hbm, out_hbm, got_ref, old_ref, out_ref, sem
):
    rep = rep_ref[0]
    pairs = [(own_hbm.at[rep], got_ref.at[0]), (old_hbm, old_ref)]
    pairs += [(src, got_ref.at[i + 1]) for i, src in enumerate((one_hbm, two_hbm, three_hbm))]
    loads = [pltpu.make_async_copy(src, dst, sem.at[i]) for i, (src, dst) in enumerate(pairs)]
    for load in loads:
        load.start()
    for load in loads:
        load.wait()
    weight = prior_weight + jnp.broadcast_to(got_ref[0, 192:193, :], (128, 128)).T
    low = iota((128, 128), 1) < 64
    for half in range(2):
        even, odd = lax.rem(rep - 2 * half + 4, 4), lax.rem(rep - 2 * half + 3, 4)
        wide0, narrow0 = got_ref[even, 0:128, :], unfold(got_ref[even, 128:192, :])
        wide1, narrow1 = got_ref[odd, 0:128, :], unfold(got_ref[odd, 128:192, :])
        turned = pltpu.roll(wide1, 64, 1)
        sums = (wide0, jnp.where(low, narrow0, turned), jnp.where(low, turned, pltpu.roll(narrow1, 64, 1)))
        for i in range(3):
            at = 384 * half + 128 * i
            out_ref[:, at : at + 128] = (prior_weight * old_ref[:, at : at + 128] + sums[i]) / weight
    store = pltpu.make_async_copy(out_ref, out_hbm, sem.at[5])
    store.start()
    store.wait()


def call(kernel, out_shape, specs, out_specs, scratch=(), flops=0, moved=0, limit=LIMIT):
    return pl.pallas_call(
        kernel,
        out_shape=out_shape,
        in_specs=specs,
        out_specs=out_specs,
        scratch_shapes=scratch,
        compiler_params=pltpu.CompilerParams(vmem_limit_bytes=limit),
        cost_estimate=pl.CostEstimate(flops=flops, bytes_accessed=moved, transcendentals=0),
    )


def shape(*dims, dtype=F32):
    return jax.ShapeDtypeStruct(dims, dtype)


def pack_call(chunk, parts, destination, labels, embeddings):
    message, count = chunk["rows"], len(chunk["owners"])
    return call(
        functools.partial(pack_kernel, chunk, parts),
        shape(128 * message, 128),
        [HBM] * 3,
        HBM,
        [
            pltpu.VMEM((1, 512), jnp.int32),
            pltpu.VMEM((1, 512), jnp.int32),
            pltpu.VMEM((512, 768), F32),
            pltpu.VMEM((132 * message, 128), F32),
            pltpu.VMEM((1024, 768), BF16),
            pltpu.VMEM((2, 256 * count // parts, 768), F32),
            DMA((3 + parts,)),
        ],
        flops=2 * 256 * count * 512 * 768 * 2,
        moved=5 * 2**20,
    )(destination, labels, embeddings)


def exchange(chunk, outgoing):
    message = chunk["rows"]
    return lax.all_to_all(
        outgoing.reshape(128, 1, message * 128), ("shard", "rep"), split_axis=0, concat_axis=0, tiled=True
    ).reshape(128 * message, 128)


def score_call(rep, received, sums, book, olds):
    return call(
        score_kernel,
        shape(32, 4096),
        [SMEM] + [HBM] * 7,
        HBM,
        [
            pltpu.VMEM((128 * ALL["rows"], 128), F32),
            pltpu.VMEM((6160, 128), F32),
            pltpu.VMEM((4, 8, 128), F32),
            pltpu.VMEM((4, 200, 128), F32),
            pltpu.VMEM((32, 256, 256), BF16),
            pltpu.VMEM((4, 192, 128), F32),
            pltpu.VMEM((208, 128), F32),
            pltpu.VMEM((4, 384, 128), F32),
            pltpu.VMEM((2, 2, 192, 2048), BF16),
            pltpu.VMEM((2, 32, 2048), F32),
            pltpu.VMEM((4, 32, 1024), F32),
            DMA((22,)),
        ],
        flops=2**32,
        moved=2**23,
        limit=SCORE_LIMIT,
    )(rep, received, sums, book, *olds)


def local(embeddings, destination, labels, old_centroids, codebook):
    rep = lax.axis_index("rep").astype(jnp.int32).reshape(1)
    destination, labels = destination.reshape(1, 512), labels.reshape(1, 512)
    outgoing = pack_call(ALL, 4, destination, labels, embeddings)
    book = call(
        book_kernel, shape(32, 256, 256, dtype=BF16), [VMEM], VMEM, flops=2**28, moved=5 * 2**20
    )(jnp.transpose(codebook, (2, 0, 1)))

    old_centroids, book = lax.optimization_barrier((old_centroids, book))
    quarters = call(
        quarters_kernel, [shape(192, 128)] * 4, [SMEM, VMEM], [VMEM] * 4, flops=2**20, moved=2**20
    )(rep, old_centroids)
    olds = [quarters[0]]
    for step in (1, 2, 3):
        olds.append(lax.ppermute(quarters[step], "rep", [(i, (i + step) % 4) for i in range(4)]))

    received = exchange(ALL, outgoing)
    received, book = lax.optimization_barrier((received, book))
    sums, *sent = call(
        sums_kernel,
        [shape(4, 200, 128)] + [shape(200, 128)] * 3,
        [SMEM, VMEM],
        [VMEM] * 4,
        flops=2**28,
        moved=2**22,
        limit=SUMS_LIMIT,
    )(rep, received)
    returned = [
        lax.ppermute(sent[step - 1], "rep", [(i, (i + step) % 4) for i in range(4)]) for step in (1, 2, 3)
    ]
    scores = score_call(rep, received, sums, book, olds)
    centroids = call(
        join_kernel,
        shape(128, 768),
        [SMEM] + [HBM] * 5,
        HBM,
        [pltpu.VMEM((4, 200, 128), F32), pltpu.VMEM((128, 768), F32), pltpu.VMEM((128, 768), F32), DMA((6,))],
        flops=2**18,
        moved=2**20,
        limit=JOIN_LIMIT,
    )(rep, sums, *returned, old_centroids)
    return (centroids, scores)


def solution(mesh):
    placed = (
        P(("shard", "rep"), None),
        P(("shard", "rep"), None),
        P(("shard", "rep")),
        P(("shard", "rep"), None),
        P("rep", None, None),
    )
    return jax.shard_map(
        local,
        mesh=mesh,
        in_specs=placed,
        out_specs=(P(("shard", "rep"), None), P("rep", "shard")),
        check_vma=False,
    )
```

```python
import functools
import jax
import jax.numpy as jnp
from jax import lax
from jax.experimental import pallas as pl
from jax.experimental.pallas import tpu as pltpu
from jax.sharding import PartitionSpec as P

prior_weight = 8.0
F32 = jnp.float32
BF16 = jnp.bfloat16
VMEM = pl.BlockSpec(memory_space=pltpu.VMEM)
SMEM = pl.BlockSpec(memory_space=pltpu.SMEM)
HBM = pl.BlockSpec(memory_space=pltpu.HBM)
DMA = pltpu.SemaphoreType.DMA
LIMIT = 58 * 2**20
SUMS_LIMIT = 24 * 2**20
SCORE_LIMIT = 48 * 2**20
JOIN_LIMIT = 16 * 2**20

ALL = {"owners": (0, 1, 2, 3), "narrow": (((0, 1), 33), ((2, 3), 41)), "labels": 0, "wide": 1, "rows": 49}


def split2(x):
    first = x.astype(BF16)
    return first, (x - first.astype(F32)).astype(BF16)


def split3(x):
    first, second = split2(x)
    third = (x - first.astype(F32) - second.astype(F32)).astype(BF16)
    return first, second, third


def iota(shape, dim):
    return lax.broadcasted_iota(jnp.int32, shape, dim)


def dot(a, b):
    return jnp.dot(a, b, preferred_element_type=F32)


def pack_kernel(
    chunk, parts, dest_hbm, label_hbm, rows_hbm, out_hbm, dest_ref, label_ref, rows_ref, out_ref, a_ref, b_ref, sem
):
    owners, message = chunk["owners"], chunk["rows"]
    count = len(owners)
    loads = [
        pltpu.make_async_copy(src, dst, sem.at[i])
        for i, (src, dst) in enumerate(((dest_hbm, dest_ref), (label_hbm, label_ref), (rows_hbm, rows_ref)))
    ]
    for load in loads:
        load.start()
    loads[0].wait()
    dest = dest_ref[...]
    named = (iota((128, 512), 0) == dest).astype(F32)
    earlier = (iota((512, 512), 0) < iota((512, 512), 1)).astype(BF16)
    before = dot(named.astype(BF16), earlier)
    spot = jnp.sum(named * before, axis=0, keepdims=True).astype(jnp.int32)
    shard, owner = dest // 4, dest % 4
    place = (owner - owners[0]) * 8 + spot
    chosen = (owner >= owners[0]) & (owner <= owners[-1])
    slot = jnp.where(chosen, shard * (8 * count) + place, -1)

    loads[1].wait()
    if chunk["labels"] is not None:
        group = (iota((32, 512), 0) == shard).astype(F32)
        within = (iota((128, 512), 0) == owner * 8 + spot).astype(BF16)
        labels = group * (label_ref[...] + 1).astype(F32)
        label_rows = lax.dot_general(
            labels.astype(BF16), within, (((1,), (1,)), ((), ())), preferred_element_type=F32
        ) - 1.0
        for quarter in range(4):
            out_ref[pl.ds(message * quarter + chunk["labels"], 32, stride=4 * message), :] = label_rows

    loads[2].wait()
    low = iota((512, 128), 1) < 64
    tile = [rows_ref[:, 128 * i : 128 * i + 128] for i in range(6)]
    wide = [
        tile[0],
        pltpu.roll(jnp.where(low, tile[2], tile[1]), 64, 1),
        tile[3],
        pltpu.roll(jnp.where(low, tile[5], tile[4]), 64, 1),
    ]
    narrow = [jnp.where(low, tile[1], tile[2]), jnp.where(low, tile[4], tile[5])]
    for i, block in enumerate(wide + narrow):
        for piece, part in enumerate(split2(block)):
            a_ref[512 * piece : 512 * piece + 512, 128 * i : 128 * i + 128] = part

    lower = iota((8, 128), 1) < 64
    stores = []
    groups = 32 // parts
    for part in range(parts):
        size = groups * 8 * count
        pick = (iota((size, 512), 0) + size * part == slot).astype(BF16)
        got = b_ref.at[part % 2]
        got[...] = dot(pick, a_ref[0:512, :]) + dot(pick, a_ref[512:1024, :])
        for s in range(groups):
            for quarter in range(4):
                base = message * (4 * (groups * part + s) + quarter)
                at = 8 * count * s
                out_ref[pl.ds(base + chunk["wide"], 8 * count), :] = got[at : at + 8 * count, 128 * quarter : 128 * quarter + 128]
                lanes = 512 + 128 * (quarter // 2)
                for members, offset in chunk["narrow"]:
                    rows = [at + 8 * (r - owners[0]) for r in members]
                    one = got[rows[0] : rows[0] + 8, lanes : lanes + 128]
                    two = got[rows[1] : rows[1] + 8, lanes : lanes + 128]
                    if quarter % 2 == 0:
                        both = jnp.where(lower, one, pltpu.roll(two, 64, 1))
                    else:
                        both = jnp.where(lower, pltpu.roll(one, 64, 1), two)
                    out_ref[pl.ds(base + offset, 8), :] = both
        span = pl.ds(128 * message // parts * part, 128 * message // parts)
        stores.append(pltpu.make_async_copy(out_ref.at[span], out_hbm.at[span], sem.at[3 + part]))
        stores[-1].start()
    for store in stores:
        store.wait()


def fold(block):
    return jnp.where(iota((64, 128), 1) < 64, block[0:64], pltpu.roll(block[64:128], 64, 1))


def unfold(block):
    return jnp.concatenate([block, pltpu.roll(block, 64, 1)], axis=0)


def quarters_kernel(rep_ref, old_ref, own_ref, one_ref, two_ref, three_ref):
    rep = rep_ref[0]
    low = iota((128, 128), 1) < 64
    tile = [old_ref[:, 128 * i : 128 * i + 128] for i in range(6)]
    wide = [
        tile[0],
        pltpu.roll(jnp.where(low, tile[2], tile[1]), 64, 1),
        tile[3],
        pltpu.roll(jnp.where(low, tile[5], tile[4]), 64, 1),
    ]
    narrow = [tile[1], pltpu.roll(tile[2], 64, 1), tile[4], pltpu.roll(tile[5], 64, 1)]
    for step, ref in enumerate((own_ref, one_ref, two_ref, three_ref)):
        which = lax.rem(rep + step, 4)
        for start, choice in ((0, wide), (128, [fold(block) for block in narrow])):
            ref[start : start + choice[0].shape[0], :] = jnp.where(
                which == 0,
                choice[0],
                jnp.where(which == 1, choice[1], jnp.where(which == 2, choice[2], choice[3])),
            )


def book_kernel(book_ref, out_ref):
    for g in range(4):
        words = book_ref[:, 8 * g : 8 * g + 8, :].reshape(48, 256)
        norm = jnp.sum((words * words).reshape(6, 8, 256), axis=0)
        first, second, third = (part.astype(F32) for part in split3(-2.0 * words))
        n1, n2, n3 = (part.astype(F32) for part in split3(norm))
        stack = jnp.concatenate([first, second, third, first, second], axis=0)
        for m in range(8):
            mine = jnp.where(iota((240, 256), 0) % 8 == m, stack, 0.0)
            tail_row = iota((16, 256), 0)
            tail = jnp.where(
                tail_row == 0,
                n1[m : m + 1],
                jnp.where(tail_row == 1, n2[m : m + 1], jnp.where(tail_row == 2, n3[m : m + 1], 0.0)),
            )
            out_ref[8 * g + m] = jnp.concatenate([mine, tail], axis=0).T.astype(BF16)


def label_rows(got_ref):
    spread = (iota((128, 512), 0) == (iota((128, 512), 1) // 128) * 8 + iota((128, 512), 1) % 8).astype(BF16)
    keep = iota((128, 512), 0) % 16 == (iota((128, 512), 1) % 128) // 8
    lab = got_ref[pl.ds(ALL["labels"], 128, stride=ALL["rows"]), :].astype(BF16)
    return jnp.sum(jnp.where(keep, dot(lab, spread), 0.0).reshape(8, 16, 512), axis=1)


def tile_rows(got_ref, c, offset):
    return jnp.concatenate([got_ref[pl.ds(ALL["rows"] * q + offset, 8), :] for q in range(16 * c, 16 * c + 16)], axis=0)


def sums_kernel(rep_ref, got_ref, sums_ref, one_ref, two_ref, three_ref):
    posting = iota((128, 128), 0).astype(F32)
    lab = label_rows(got_ref)
    sums = [None] * 4
    counts = [None] * 4
    for c in range(8):
        for members, offset in ALL["narrow"]:
            narrow_parts = split2(tile_rows(got_ref, c, offset))
            for r in members:
                hot = (posting == lab[c : c + 1, 128 * r : 128 * r + 128]).astype(F32)
                right = jnp.concatenate(
                    [
                        jnp.concatenate([a, b], axis=1)
                        for a, b in zip(split2(tile_rows(got_ref, c, ALL["wide"] + 8 * r)), narrow_parts)
                    ],
                    axis=0,
                )
                left = hot.astype(BF16)
                total = dot(jnp.concatenate([left, left], axis=1), right)
                sums[r] = total if sums[r] is None else sums[r] + total
                counts[r] = hot if counts[r] is None else counts[r] + hot
    for members, _ in ALL["narrow"]:
        for k, r in enumerate(members):
            tail = sums[r][:, 128:256]
            if k:
                tail = pltpu.roll(tail, 64, 1)
            sums_ref[r, 0:128, :] = sums[r][:, 0:128]
            sums_ref[r, 128:192, :] = fold(tail)
            sums_ref[r, 192:200, :] = jnp.broadcast_to(jnp.sum(counts[r].T, axis=0, keepdims=True), (8, 128))
    for step, ref in ((1, one_ref), (2, two_ref), (3, three_ref)):
        ref[...] = sums_ref[lax.rem(rep_ref[0] + step, 4)]


def score_kernel(
    rep_ref, got_ref, sums_hbm, book_hbm, own_hbm, one_hbm, two_hbm, three_hbm, out_hbm,
    work_ref, lab_ref, sums_ref, book_ref, old_ref, flip_ref, cent_ref, piece_ref, norm_ref, out_ref, sem,
):
    def fetch(src, dst, at):
        return pltpu.make_async_copy(src, dst, sem.at[at])

    def fetch_book(g):
        return fetch(book_hbm.at[pl.ds(8 * g, 8)], book_ref.at[pl.ds(8 * g, 8)], 4 + g)

    def send(g):
        span = pl.ds(8 * g, 8)
        return fetch(out_ref.at[span], out_hbm.at[span], 14 + g)

    small = [fetch(sums_hbm, sums_ref, 8)]
    small += [fetch(src, old_ref.at[i], 10 + i) for i, src in enumerate((own_hbm, one_hbm, two_hbm, three_hbm))]
    for copy in small:
        copy.start()
    for g in range(4):
        fetch_book(g).start()
    rep = rep_ref[0]
    for c in range(8):
        for members, offset in ALL["narrow"]:
            narrow = tile_rows(got_ref, c, offset).T
            for k, r in enumerate(members):
                at = 192 * (8 * r + c)
                work_ref[at : at + 128, :] = tile_rows(got_ref, c, ALL["wide"] + 8 * r).T
                work_ref[at + 128 : at + 192, :] = narrow[64 * k : 64 * k + 64]
    lab = label_rows(got_ref)
    for copy in small:
        copy.wait()
    for r in range(4):
        lab_ref[r] = lab[:, 128 * r : 128 * r + 128]
        total = prior_weight * old_ref[lax.rem(rep - r + 4, 4)] + sums_ref[r, 0:192, :]
        weight = prior_weight + sums_ref[r, 192:193, :]
        flip_ref[0:128, :] = total[0:128].T / weight
        flip_ref[128:192, :] = unfold(total[128:192]).T[0:64] / weight
        for g in range(4):
            for t in range(6):
                for piece, block in enumerate(split2(flip_ref[pl.ds(48 * g + t, 8, stride=6), :])):
                    at = 192 * piece + 48 * g + 8 * t
                    cent_ref[r, at : at + 8, :] = block.astype(F32)

    def prepare(r):
        labs = lab_ref[r]
        lanes = slice(1024 * r, 1024 * r + 1024)
        posting = iota((128, 128), 0).astype(F32)
        hot = jnp.concatenate([(posting == labs[c : c + 1]).astype(BF16) for c in range(8)], axis=1)
        near = dot(cent_ref[r].astype(BF16), hot)
        for g in range(4):
            span = slice(48 * g, 48 * g + 48)
            rows = jnp.concatenate(
                [
                    jnp.concatenate(
                        [work_ref[pl.ds(192 * (8 * r + c) + 48 * g + t, 8, stride=6), :] for c in range(8)], axis=1
                    )
                    for t in range(6)
                ],
                axis=0,
            )
            res = rows - (near[span] + near[192 + 48 * g : 240 + 48 * g])
            norm_ref[8 * g : 8 * g + 8, lanes] = jnp.sum((res * res).reshape(6, 8, 1024), axis=0)
            for i, piece in enumerate(split2(res)):
                piece_ref[i, span, lanes] = piece

    ones = jnp.where(iota((16, 4096), 0) < 3, 1.0, 0.0).astype(BF16)

    def score(g):
        first = piece_ref[0, 48 * g : 48 * g + 48, :]
        second = piece_ref[1, 48 * g : 48 * g + 48, :]
        right = jnp.concatenate([first, first, first, second, second, ones], axis=0)
        best = []
        for m in range(8):
            value = dot(book_ref[8 * g + m], right)
            value = jnp.min(value.reshape(32, 8, 4096), axis=0)
            best.append(jnp.min(value, axis=0, keepdims=True))
        out_ref[8 * g : 8 * g + 8, :] = jnp.concatenate(best, axis=0) + norm_ref[8 * g : 8 * g + 8, :]

    for r in range(4):
        prepare(r)
    for g in range(4):
        fetch_book(g).wait()
    for g in range(4):
        score(g)
        send(g).start()
    for g in range(4):
        send(g).wait()


def join_kernel(
    rep_ref, own_hbm, one_hbm, two_hbm, three_hbm, old_hbm, out_hbm, got_ref, old_ref, out_ref, sem
):
    rep = rep_ref[0]
    pairs = [(own_hbm.at[rep], got_ref.at[0]), (old_hbm, old_ref)]
    pairs += [(src, got_ref.at[i + 1]) for i, src in enumerate((one_hbm, two_hbm, three_hbm))]
    loads = [pltpu.make_async_copy(src, dst, sem.at[i]) for i, (src, dst) in enumerate(pairs)]
    for load in loads:
        load.start()
    for load in loads:
        load.wait()
    weight = prior_weight + jnp.broadcast_to(got_ref[0, 192:193, :], (128, 128)).T
    low = iota((128, 128), 1) < 64
    for half in range(2):
        even, odd = lax.rem(rep - 2 * half + 4, 4), lax.rem(rep - 2 * half + 3, 4)
        wide0, narrow0 = got_ref[even, 0:128, :], unfold(got_ref[even, 128:192, :])
        wide1, narrow1 = got_ref[odd, 0:128, :], unfold(got_ref[odd, 128:192, :])
        turned = pltpu.roll(wide1, 64, 1)
        sums = (wide0, jnp.where(low, narrow0, turned), jnp.where(low, turned, pltpu.roll(narrow1, 64, 1)))
        for i in range(3):
            at = 384 * half + 128 * i
            out_ref[:, at : at + 128] = (prior_weight * old_ref[:, at : at + 128] + sums[i]) / weight
    store = pltpu.make_async_copy(out_ref, out_hbm, sem.at[5])
    store.start()
    store.wait()


def call(kernel, out_shape, specs, out_specs, scratch=(), flops=0, moved=0, limit=LIMIT):
    return pl.pallas_call(
        kernel,
        out_shape=out_shape,
        in_specs=specs,
        out_specs=out_specs,
        scratch_shapes=scratch,
        compiler_params=pltpu.CompilerParams(vmem_limit_bytes=limit),
        cost_estimate=pl.CostEstimate(flops=flops, bytes_accessed=moved, transcendentals=0),
    )


def shape(*dims, dtype=F32):
    return jax.ShapeDtypeStruct(dims, dtype)


def pack_call(chunk, parts, destination, labels, embeddings):
    message, count = chunk["rows"], len(chunk["owners"])
    return call(
        functools.partial(pack_kernel, chunk, parts),
        shape(128 * message, 128),
        [HBM] * 3,
        HBM,
        [
            pltpu.VMEM((1, 512), jnp.int32),
            pltpu.VMEM((1, 512), jnp.int32),
            pltpu.VMEM((512, 768), F32),
            pltpu.VMEM((132 * message, 128), F32),
            pltpu.VMEM((1024, 768), BF16),
            pltpu.VMEM((2, 256 * count // parts, 768), F32),
            DMA((3 + parts,)),
        ],
        flops=2 * 256 * count * 512 * 768 * 2,
        moved=5 * 2**20,
    )(destination, labels, embeddings)


def exchange(chunk, outgoing):
    message = chunk["rows"]
    return lax.all_to_all(
        outgoing.reshape(128, 1, message * 128), ("shard", "rep"), split_axis=0, concat_axis=0, tiled=True
    ).reshape(128 * message, 128)


def score_call(rep, received, sums, book, olds):
    return call(
        score_kernel,
        shape(32, 4096),
        [SMEM, VMEM] + [HBM] * 6,
        HBM,
        [
            pltpu.VMEM((6160, 128), F32),
            pltpu.VMEM((4, 8, 128), F32),
            pltpu.VMEM((4, 200, 128), F32),
            pltpu.VMEM((32, 256, 256), BF16),
            pltpu.VMEM((4, 192, 128), F32),
            pltpu.VMEM((208, 128), F32),
            pltpu.VMEM((4, 384, 128), F32),
            pltpu.VMEM((2, 192, 4096), BF16),
            pltpu.VMEM((32, 4096), F32),
            pltpu.VMEM((32, 4096), F32),
            DMA((22,)),
        ],
        flops=2**32,
        moved=2**23,
        limit=SCORE_LIMIT,
    )(rep, received, sums, book, *olds)


def local(embeddings, destination, labels, old_centroids, codebook):
    rep = lax.axis_index("rep").astype(jnp.int32).reshape(1)
    destination, labels = destination.reshape(1, 512), labels.reshape(1, 512)
    outgoing = pack_call(ALL, 4, destination, labels, embeddings)
    book = call(
        book_kernel, shape(32, 256, 256, dtype=BF16), [VMEM], VMEM, flops=2**28, moved=5 * 2**20
    )(jnp.transpose(codebook, (2, 0, 1)))

    old_centroids, book = lax.optimization_barrier((old_centroids, book))
    quarters = call(
        quarters_kernel, [shape(192, 128)] * 4, [SMEM, VMEM], [VMEM] * 4, flops=2**20, moved=2**20
    )(rep, old_centroids)
    olds = [quarters[0]]
    for step in (1, 2, 3):
        olds.append(lax.ppermute(quarters[step], "rep", [(i, (i + step) % 4) for i in range(4)]))

    received = exchange(ALL, outgoing)
    received, book = lax.optimization_barrier((received, book))
    sums, *sent = call(
        sums_kernel,
        [shape(4, 200, 128)] + [shape(200, 128)] * 3,
        [SMEM, VMEM],
        [VMEM] * 4,
        flops=2**28,
        moved=2**22,
        limit=SUMS_LIMIT,
    )(rep, received)
    returned = [
        lax.ppermute(sent[step - 1], "rep", [(i, (i + step) % 4) for i in range(4)]) for step in (1, 2, 3)
    ]
    scores = score_call(rep, received, sums, book, olds)
    centroids = call(
        join_kernel,
        shape(128, 768),
        [SMEM] + [HBM] * 5,
        HBM,
        [pltpu.VMEM((4, 200, 128), F32), pltpu.VMEM((128, 768), F32), pltpu.VMEM((128, 768), F32), DMA((6,))],
        flops=2**18,
        moved=2**20,
        limit=JOIN_LIMIT,
    )(rep, sums, *returned, old_centroids)
    return (centroids, scores)


def solution(mesh):
    placed = (
        P(("shard", "rep"), None),
        P(("shard", "rep"), None),
        P(("shard", "rep")),
        P(("shard", "rep"), None),
        P("rep", None, None),
    )
    return jax.shard_map(
        local,
        mesh=mesh,
        in_specs=placed,
        out_specs=(P(("shard", "rep"), None), P("rep", "shard")),
        check_vma=False,
    )
```

```python
import functools
import jax
import jax.numpy as jnp
from jax import lax
from jax.experimental import pallas as pl
from jax.experimental.pallas import tpu as pltpu
from jax.sharding import PartitionSpec as P

prior_weight = 8.0
F32 = jnp.float32
BF16 = jnp.bfloat16
VMEM = pl.BlockSpec(memory_space=pltpu.VMEM)
SMEM = pl.BlockSpec(memory_space=pltpu.SMEM)
HBM = pl.BlockSpec(memory_space=pltpu.HBM)
DMA = pltpu.SemaphoreType.DMA
LIMIT = 58 * 2**20
SUMS_LIMIT = 24 * 2**20
SCORE_LIMIT = 48 * 2**20
JOIN_LIMIT = 16 * 2**20

ALL = {"owners": (0, 1, 2, 3), "narrow": (((0, 1), 33), ((2, 3), 41)), "labels": 0, "wide": 1, "rows": 49}


def split2(x):
    first = x.astype(BF16)
    return first, (x - first.astype(F32)).astype(BF16)


def split3(x):
    first, second = split2(x)
    third = (x - first.astype(F32) - second.astype(F32)).astype(BF16)
    return first, second, third


def iota(shape, dim):
    return lax.broadcasted_iota(jnp.int32, shape, dim)


def dot(a, b):
    return jnp.dot(a, b, preferred_element_type=F32)


def pack_kernel(
    chunk, parts, dest_hbm, label_hbm, rows_hbm, out_hbm, dest_ref, label_ref, rows_ref, out_ref, a_ref, b_ref, sem
):
    owners, message = chunk["owners"], chunk["rows"]
    count = len(owners)
    loads = [
        pltpu.make_async_copy(src, dst, sem.at[i])
        for i, (src, dst) in enumerate(((dest_hbm, dest_ref), (label_hbm, label_ref), (rows_hbm, rows_ref)))
    ]
    for load in loads:
        load.start()
    loads[0].wait()
    dest = dest_ref[...]
    named = (iota((128, 512), 0) == dest).astype(F32)
    earlier = (iota((512, 512), 0) < iota((512, 512), 1)).astype(BF16)
    before = dot(named.astype(BF16), earlier)
    spot = jnp.sum(named * before, axis=0, keepdims=True).astype(jnp.int32)
    shard, owner = dest // 4, dest % 4
    place = (owner - owners[0]) * 8 + spot
    chosen = (owner >= owners[0]) & (owner <= owners[-1])
    slot = jnp.where(chosen, shard * (8 * count) + place, -1)

    loads[1].wait()
    if chunk["labels"] is not None:
        group = (iota((32, 512), 0) == shard).astype(F32)
        within = (iota((128, 512), 0) == owner * 8 + spot).astype(BF16)
        labels = group * (label_ref[...] + 1).astype(F32)
        label_rows = lax.dot_general(
            labels.astype(BF16), within, (((1,), (1,)), ((), ())), preferred_element_type=F32
        ) - 1.0
        for quarter in range(4):
            out_ref[pl.ds(message * quarter + chunk["labels"], 32, stride=4 * message), :] = label_rows

    loads[2].wait()
    low = iota((512, 128), 1) < 64
    tile = [rows_ref[:, 128 * i : 128 * i + 128] for i in range(6)]
    wide = [
        tile[0],
        pltpu.roll(jnp.where(low, tile[2], tile[1]), 64, 1),
        tile[3],
        pltpu.roll(jnp.where(low, tile[5], tile[4]), 64, 1),
    ]
    narrow = [jnp.where(low, tile[1], tile[2]), jnp.where(low, tile[4], tile[5])]
    for i, block in enumerate(wide + narrow):
        for piece, part in enumerate(split2(block)):
            a_ref[512 * piece : 512 * piece + 512, 128 * i : 128 * i + 128] = part

    lower = iota((8, 128), 1) < 64
    stores = []
    groups = 32 // parts
    for part in range(parts):
        size = groups * 8 * count
        pick = (iota((size, 512), 0) + size * part == slot).astype(BF16)
        got = b_ref.at[part % 2]
        got[...] = dot(pick, a_ref[0:512, :]) + dot(pick, a_ref[512:1024, :])
        for s in range(groups):
            for quarter in range(4):
                base = message * (4 * (groups * part + s) + quarter)
                at = 8 * count * s
                out_ref[pl.ds(base + chunk["wide"], 8 * count), :] = got[at : at + 8 * count, 128 * quarter : 128 * quarter + 128]
                lanes = 512 + 128 * (quarter // 2)
                for members, offset in chunk["narrow"]:
                    rows = [at + 8 * (r - owners[0]) for r in members]
                    one = got[rows[0] : rows[0] + 8, lanes : lanes + 128]
                    two = got[rows[1] : rows[1] + 8, lanes : lanes + 128]
                    if quarter % 2 == 0:
                        both = jnp.where(lower, one, pltpu.roll(two, 64, 1))
                    else:
                        both = jnp.where(lower, pltpu.roll(one, 64, 1), two)
                    out_ref[pl.ds(base + offset, 8), :] = both
        span = pl.ds(128 * message // parts * part, 128 * message // parts)
        stores.append(pltpu.make_async_copy(out_ref.at[span], out_hbm.at[span], sem.at[3 + part]))
        stores[-1].start()
    for store in stores:
        store.wait()


def fold(block):
    return jnp.where(iota((64, 128), 1) < 64, block[0:64], pltpu.roll(block[64:128], 64, 1))


def unfold(block):
    return jnp.concatenate([block, pltpu.roll(block, 64, 1)], axis=0)


def quarters_kernel(rep_ref, old_ref, own_ref, one_ref, two_ref, three_ref):
    rep = rep_ref[0]
    low = iota((128, 128), 1) < 64
    tile = [old_ref[:, 128 * i : 128 * i + 128] for i in range(6)]
    wide = [
        tile[0],
        pltpu.roll(jnp.where(low, tile[2], tile[1]), 64, 1),
        tile[3],
        pltpu.roll(jnp.where(low, tile[5], tile[4]), 64, 1),
    ]
    narrow = [tile[1], pltpu.roll(tile[2], 64, 1), tile[4], pltpu.roll(tile[5], 64, 1)]
    for step, ref in enumerate((own_ref, one_ref, two_ref, three_ref)):
        which = lax.rem(rep + step, 4)
        for start, choice in ((0, wide), (128, [fold(block) for block in narrow])):
            ref[start : start + choice[0].shape[0], :] = jnp.where(
                which == 0,
                choice[0],
                jnp.where(which == 1, choice[1], jnp.where(which == 2, choice[2], choice[3])),
            )


def book_kernel(book_ref, out_ref):
    for g in range(4):
        words = book_ref[:, 8 * g : 8 * g + 8, :].reshape(48, 256)
        norm = jnp.sum((words * words).reshape(6, 8, 256), axis=0)
        first, second, third = (part.astype(F32) for part in split3(-2.0 * words))
        n1, n2, n3 = (part.astype(F32) for part in split3(norm))
        stack = jnp.concatenate([first, second, third, first, second], axis=0)
        for m in range(8):
            mine = jnp.where(iota((240, 256), 0) % 8 == m, stack, 0.0)
            tail_row = iota((16, 256), 0)
            tail = jnp.where(
                tail_row == 0,
                n1[m : m + 1],
                jnp.where(tail_row == 1, n2[m : m + 1], jnp.where(tail_row == 2, n3[m : m + 1], 0.0)),
            )
            out_ref[8 * g + m] = jnp.concatenate([mine, tail], axis=0).T.astype(BF16)


def label_rows(got_ref):
    spread = (iota((128, 512), 0) == (iota((128, 512), 1) // 128) * 8 + iota((128, 512), 1) % 8).astype(BF16)
    keep = iota((128, 512), 0) % 16 == (iota((128, 512), 1) % 128) // 8
    lab = got_ref[pl.ds(ALL["labels"], 128, stride=ALL["rows"]), :].astype(BF16)
    return jnp.sum(jnp.where(keep, dot(lab, spread), 0.0).reshape(8, 16, 512), axis=1)


def tile_rows(got_ref, c, offset):
    return jnp.concatenate([got_ref[pl.ds(ALL["rows"] * q + offset, 8), :] for q in range(16 * c, 16 * c + 16)], axis=0)


def sums_kernel(rep_ref, got_ref, sums_ref, one_ref, two_ref, three_ref):
    posting = iota((128, 128), 0).astype(F32)
    lab = label_rows(got_ref)
    sums = [None] * 4
    counts = [None] * 4
    for c in range(8):
        for members, offset in ALL["narrow"]:
            narrow_parts = split2(tile_rows(got_ref, c, offset))
            for r in members:
                hot = (posting == lab[c : c + 1, 128 * r : 128 * r + 128]).astype(F32)
                right = jnp.concatenate(
                    [
                        jnp.concatenate([a, b], axis=1)
                        for a, b in zip(split2(tile_rows(got_ref, c, ALL["wide"] + 8 * r)), narrow_parts)
                    ],
                    axis=0,
                )
                left = hot.astype(BF16)
                total = dot(jnp.concatenate([left, left], axis=1), right)
                sums[r] = total if sums[r] is None else sums[r] + total
                counts[r] = hot if counts[r] is None else counts[r] + hot
    for members, _ in ALL["narrow"]:
        for k, r in enumerate(members):
            tail = sums[r][:, 128:256]
            if k:
                tail = pltpu.roll(tail, 64, 1)
            sums_ref[r, 0:128, :] = sums[r][:, 0:128]
            sums_ref[r, 128:192, :] = fold(tail)
            sums_ref[r, 192:200, :] = jnp.broadcast_to(jnp.sum(counts[r].T, axis=0, keepdims=True), (8, 128))
    for step, ref in ((1, one_ref), (2, two_ref), (3, three_ref)):
        ref[...] = sums_ref[lax.rem(rep_ref[0] + step, 4)]


def score_kernel(
    rep_ref, got_ref, sums_hbm, book_hbm, own_hbm, one_hbm, two_hbm, three_hbm, out_hbm,
    work_ref, lab_ref, sums_ref, book_ref, old_ref, flip_ref, cent_ref, piece_ref, norm_ref, out_ref, sem,
):
    def fetch(src, dst, at):
        return pltpu.make_async_copy(src, dst, sem.at[at])

    def fetch_book(g):
        return fetch(book_hbm.at[pl.ds(8 * g, 8)], book_ref.at[pl.ds(8 * g, 8)], 4 + g)

    def send(g):
        span = pl.ds(8 * g, 8)
        return fetch(out_ref.at[span], out_hbm.at[span], 14 + g)

    small = [fetch(sums_hbm, sums_ref, 8)]
    small += [fetch(src, old_ref.at[i], 10 + i) for i, src in enumerate((own_hbm, one_hbm, two_hbm, three_hbm))]
    for copy in small:
        copy.start()
    for g in range(4):
        fetch_book(g).start()
    rep = rep_ref[0]
    for c in range(8):
        for members, offset in ALL["narrow"]:
            narrow = tile_rows(got_ref, c, offset).T
            for k, r in enumerate(members):
                at = 192 * (8 * r + c)
                work_ref[at : at + 128, :] = tile_rows(got_ref, c, ALL["wide"] + 8 * r).T
                work_ref[at + 128 : at + 192, :] = narrow[64 * k : 64 * k + 64]
    lab = label_rows(got_ref)
    for copy in small:
        copy.wait()
    for r in range(4):
        lab_ref[r] = lab[:, 128 * r : 128 * r + 128]
        total = prior_weight * old_ref[lax.rem(rep - r + 4, 4)] + sums_ref[r, 0:192, :]
        weight = prior_weight + sums_ref[r, 192:193, :]
        flip_ref[0:128, :] = total[0:128].T / weight
        flip_ref[128:192, :] = unfold(total[128:192]).T[0:64] / weight
        for g in range(4):
            for t in range(6):
                for piece, block in enumerate(split2(flip_ref[pl.ds(48 * g + t, 8, stride=6), :])):
                    at = 192 * piece + 48 * g + 8 * t
                    cent_ref[r, at : at + 8, :] = block.astype(F32)

    def prepare(r):
        labs = lab_ref[r]
        lanes = slice(1024 * r, 1024 * r + 1024)
        posting = iota((128, 128), 0).astype(F32)
        hot = jnp.concatenate([(posting == labs[c : c + 1]).astype(BF16) for c in range(8)], axis=1)
        near = dot(cent_ref[r].astype(BF16), hot)
        for g in range(4):
            span = slice(48 * g, 48 * g + 48)
            rows = jnp.concatenate(
                [
                    jnp.concatenate(
                        [work_ref[pl.ds(192 * (8 * r + c) + 48 * g + t, 8, stride=6), :] for c in range(8)], axis=1
                    )
                    for t in range(6)
                ],
                axis=0,
            )
            res = rows - (near[span] + near[192 + 48 * g : 240 + 48 * g])
            norm_ref[8 * g : 8 * g + 8, lanes] = jnp.sum((res * res).reshape(6, 8, 1024), axis=0)
            for i, piece in enumerate(split2(res)):
                piece_ref[i, span, lanes] = piece

    ones = jnp.where(iota((16, 4096), 0) < 3, 1.0, 0.0).astype(BF16)

    def score(g):
        first = piece_ref[0, 48 * g : 48 * g + 48, :]
        second = piece_ref[1, 48 * g : 48 * g + 48, :]
        right = jnp.concatenate([first, first, first, second, second, ones], axis=0)
        best = []
        for m in range(8):
            value = dot(book_ref[8 * g + m], right)
            value = jnp.min(value.reshape(32, 8, 4096), axis=0)
            best.append(jnp.min(value, axis=0, keepdims=True))
        out_ref[8 * g : 8 * g + 8, :] = jnp.concatenate(best, axis=0) + norm_ref[8 * g : 8 * g + 8, :]

    for r in range(4):
        prepare(r)
    for g in range(4):
        fetch_book(g).wait()
    for g in range(4):
        score(g)
        send(g).start()
    for g in range(4):
        send(g).wait()


def join_kernel(
    rep_ref, own_hbm, one_hbm, two_hbm, three_hbm, old_hbm, out_hbm, got_ref, old_ref, out_ref, sem
):
    rep = rep_ref[0]
    pairs = [(own_hbm.at[rep], got_ref.at[0]), (old_hbm, old_ref)]
    pairs += [(src, got_ref.at[i + 1]) for i, src in enumerate((one_hbm, two_hbm, three_hbm))]
    loads = [pltpu.make_async_copy(src, dst, sem.at[i]) for i, (src, dst) in enumerate(pairs)]
    for load in loads:
        load.start()
    for load in loads:
        load.wait()
    weight = prior_weight + jnp.broadcast_to(got_ref[0, 192:193, :], (128, 128)).T
    low = iota((128, 128), 1) < 64
    for half in range(2):
        even, odd = lax.rem(rep - 2 * half + 4, 4), lax.rem(rep - 2 * half + 3, 4)
        wide0, narrow0 = got_ref[even, 0:128, :], unfold(got_ref[even, 128:192, :])
        wide1, narrow1 = got_ref[odd, 0:128, :], unfold(got_ref[odd, 128:192, :])
        turned = pltpu.roll(wide1, 64, 1)
        sums = (wide0, jnp.where(low, narrow0, turned), jnp.where(low, turned, pltpu.roll(narrow1, 64, 1)))
        for i in range(3):
            at = 384 * half + 128 * i
            out_ref[:, at : at + 128] = (prior_weight * old_ref[:, at : at + 128] + sums[i]) / weight
    store = pltpu.make_async_copy(out_ref, out_hbm, sem.at[5])
    store.start()
    store.wait()


def call(kernel, out_shape, specs, out_specs, scratch=(), flops=0, moved=0, limit=LIMIT):
    return pl.pallas_call(
        kernel,
        out_shape=out_shape,
        in_specs=specs,
        out_specs=out_specs,
        scratch_shapes=scratch,
        compiler_params=pltpu.CompilerParams(vmem_limit_bytes=limit),
        cost_estimate=pl.CostEstimate(flops=flops, bytes_accessed=moved, transcendentals=0),
    )


def shape(*dims, dtype=F32):
    return jax.ShapeDtypeStruct(dims, dtype)


def pack_call(chunk, parts, destination, labels, embeddings):
    message, count = chunk["rows"], len(chunk["owners"])
    return call(
        functools.partial(pack_kernel, chunk, parts),
        shape(128 * message, 128),
        [HBM] * 3,
        HBM,
        [
            pltpu.VMEM((1, 512), jnp.int32),
            pltpu.VMEM((1, 512), jnp.int32),
            pltpu.VMEM((512, 768), F32),
            pltpu.VMEM((132 * message, 128), F32),
            pltpu.VMEM((1024, 768), BF16),
            pltpu.VMEM((2, 256 * count // parts, 768), F32),
            DMA((3 + parts,)),
        ],
        flops=2 * 256 * count * 512 * 768 * 2,
        moved=5 * 2**20,
    )(destination, labels, embeddings)


def exchange(chunk, outgoing):
    message = chunk["rows"]
    return lax.all_to_all(
        outgoing.reshape(128, 1, message * 128), ("shard", "rep"), split_axis=0, concat_axis=0, tiled=True
    ).reshape(128 * message, 128)


def score_call(rep, received, sums, book, olds):
    return call(
        score_kernel,
        shape(32, 4096),
        [SMEM, VMEM] + [HBM] * 6,
        HBM,
        [
            pltpu.VMEM((6160, 128), F32),
            pltpu.VMEM((4, 8, 128), F32),
            pltpu.VMEM((4, 200, 128), F32),
            pltpu.VMEM((32, 256, 256), BF16),
            pltpu.VMEM((4, 192, 128), F32),
            pltpu.VMEM((208, 128), F32),
            pltpu.VMEM((4, 384, 128), F32),
            pltpu.VMEM((2, 192, 4096), BF16),
            pltpu.VMEM((32, 4096), F32),
            pltpu.VMEM((32, 4096), F32),
            DMA((22,)),
        ],
        flops=2**32,
        moved=2**23,
        limit=SCORE_LIMIT,
    )(rep, received, sums, book, *olds)


def local(embeddings, destination, labels, old_centroids, codebook):
    rep = lax.axis_index("rep").astype(jnp.int32).reshape(1)
    destination, labels = destination.reshape(1, 512), labels.reshape(1, 512)
    outgoing = pack_call(ALL, 4, destination, labels, embeddings)
    book = call(
        book_kernel, shape(32, 256, 256, dtype=BF16), [VMEM], VMEM, flops=2**28, moved=5 * 2**20
    )(jnp.transpose(codebook, (2, 0, 1)))

    quarters = call(
        quarters_kernel, [shape(192, 128)] * 4, [SMEM, VMEM], [VMEM] * 4, flops=2**20, moved=2**20
    )(rep, old_centroids)
    olds = [quarters[0]]
    for step in (1, 2, 3):
        olds.append(lax.ppermute(quarters[step], "rep", [(i, (i + step) % 4) for i in range(4)]))

    received = exchange(ALL, outgoing)
    received, book = lax.optimization_barrier((received, book))
    sums, *sent = call(
        sums_kernel,
        [shape(4, 200, 128)] + [shape(200, 128)] * 3,
        [SMEM, VMEM],
        [VMEM] * 4,
        flops=2**28,
        moved=2**22,
        limit=SUMS_LIMIT,
    )(rep, received)
    returned = [
        lax.ppermute(sent[step - 1], "rep", [(i, (i + step) % 4) for i in range(4)]) for step in (1, 2, 3)
    ]
    scores = score_call(rep, received, sums, book, olds)
    centroids = call(
        join_kernel,
        shape(128, 768),
        [SMEM] + [HBM] * 5,
        HBM,
        [pltpu.VMEM((4, 200, 128), F32), pltpu.VMEM((128, 768), F32), pltpu.VMEM((128, 768), F32), DMA((6,))],
        flops=2**18,
        moved=2**20,
        limit=JOIN_LIMIT,
    )(rep, sums, *returned, old_centroids)
    return (centroids, scores)


def solution(mesh):
    placed = (
        P(("shard", "rep"), None),
        P(("shard", "rep"), None),
        P(("shard", "rep")),
        P(("shard", "rep"), None),
        P("rep", None, None),
    )
    return jax.shard_map(
        local,
        mesh=mesh,
        in_specs=placed,
        out_specs=(P(("shard", "rep"), None), P("rep", "shard")),
        check_vma=False,
    )
```
